32 devices in a mesh: seq: 16 (over z, y, x), tp: 2 (over core).
Axes of the slice: x: 2, y: 2, z: 4, core: 2. Of those that a mesh axis runs over, the one named last changes fastest.
Arguments:
- hidden_in: bfloat16 [4096, 1536], P('seq'), may hold values from -6 to 6
- gate_proj: float32 [1536, 3072], P(('seq', 'tp')), may hold values from -0.15625 to 0.15625
- inner_proj: float32 [1536, 3072], P(('seq', 'tp')), may hold values from -0.15625 to 0.15625
- small_proj: float32 [1536, 304], P(('seq', 'tp')), may hold values from -0.15625 to 0.15625
- row_layout: int32 [32], replicated, may hold values from 0 to 31, each once
- conv_inner: float32 [4, 3072], P(None, 'tp'), may hold values from -3 to 3
- conv_shared: float32 [4, 256], replicated, may hold values from -3 to 3
- bias_inner: float32 [3072], P('tp'), may hold values from -3 to 3
- bias_shared: float32 [256], replicated, may hold values from -3 to 3
- dt_bias: float32 [48], P('tp'), may hold values from -4 to -1
- decay_log: float32 [48], P('tp'), may hold values from -8 to 0
- skip_gain: float32 [48], P('tp'), may hold values from 0.5 to 2
- norm_gain: float32 [3072], P('tp'), may hold values from 0.1 to 1.9
- out_proj: float32 [3072, 1536], P('tp', 'seq'), may hold values from -0.109375 to 0.109375
- prompt_lengths: int32 [8], replicated, may hold values from 1 to 2048, 4096 in all
- group_map: int32 [8], replicated, may hold values from 0 to 3
- init_states: float32 [4, 48, 64, 128], P(None, 'tp'), may hold values from -12 to 12
- page_table: int32 [32], P('seq'), may hold values from 0 to 31, as said below
Outputs:
- mixed_out: bfloat16 [4096, 1536], P(('seq', 'tp'))
- state_pages: float32 [32, 48, 64, 128], P('seq', 'tp')
The draws below stay inside these ranges and needn't reach their ends.
Inputs may be any that keep to these rules, and one draw needn't show every extreme that they name: `prompt_lengths`: the lengths sum to 4096; the longest prompt has exactly 2048 tokens. `row_layout`: a permutation. `page_table`: no two snapshots share a slot; snapshot k goes to one of the 2 slots of the aligned block of 2 snapshots that holds k.
All inputs are finite; a program needn't handle non-finite values.
Results may differ from the reference program's by a relative error of at most 0.018.
Values may be sent and summed in bfloat16 or wider, within the bound.
No kernel may reach another device: no remote copies, remote signals or barrier semaphores. Data moves between devices by JAX's collectives and lax.ppermute only.
A program may use at most 192 MiB of HBM per device.

```python
import math
import jax
import jax.numpy as jnp
import numpy as np
from jax import lax

D = 1536
H = 48
P_SIZE = 64
N = 128
CONV = 4
PAGE = 128
GROUPS = 4
PROMPTS = 8
DI = 3072
TOKENS = 4096
MOST = 2048
PAGE_DEV = 2
PAGES = 32
BLOCKS = 32


def draw_page_table(key, part):
    block_count = PAGES // PAGE_DEV
    keys = jax.random.split(jax.random.fold_in(key, 17), block_count)
    orders = jax.vmap(lambda one_key: jax.random.permutation(one_key, PAGE_DEV))(keys)
    base = jnp.arange(block_count, dtype=jnp.int32)[:, None] * PAGE_DEV
    return (orders.astype(jnp.int32) + base).reshape(PAGES).astype(jnp.int32)


def set_ends(array, rng, smallest, top_value):
    spot = [jax.random.randint(jax.random.fold_in(rng, axis), (), 0, length) for axis, length in enumerate(array.shape)]
    main_axis = array.shape.index(max(array.shape))
    neighbour = spot[:main_axis] + [(spot[main_axis] + 1) % array.shape[main_axis]] + spot[main_axis + 1:]
    return array.at[tuple(spot)].set(smallest).at[tuple(neighbour)].set(top_value)


def levels(key, extent, cuts, least, largest):
    factor_of = 1.0
    for dim, blocks in cuts:
        draws = jax.random.uniform(jax.random.fold_in(jax.random.fold_in(key, 6), dim), (blocks,), jnp.float32, least / len(cuts), largest / len(cuts))
        factor_of = factor_of * jnp.repeat(jnp.exp(draws), extent[dim] // blocks).reshape((-1,) + (1,) * (len(extent) - 1 - dim))
    return factor_of


def split_up(count, total, bound, skew):
    portions = [(1 << 20) // math.isqrt(rank ** skew) + 1 for rank in range(2, count + 1)]
    rest, given = total - bound - (count - 1), [1] * (count - 1)
    while rest > 0:
        free = [i for i in range(count - 1) if given[i] < bound]
        whole, budget = sum([portions[i] for i in free]), rest
        for i in free:
            extra = min(bound - given[i], max(1, budget * portions[i] // whole), rest)
            given[i] = given[i] + extra
            rest = rest - extra
    return np.array([bound] + given)


def ragged(stream_key, number_of, total, reach, lean):
    if number_of == 2:
        one = jax.random.randint(stream_key, (), max(1, total - reach), min(reach, total - 1) + 1)
        return jnp.stack([one, total - one])
    sizes = jnp.asarray(split_up(number_of, total, reach, lean), jnp.int32)
    pairs = (number_of - 1) // 2
    giver, taker = sizes[1:1 + 2 * pairs:2], sizes[2:2 + 2 * pairs:2]
    room = jnp.minimum(giver - 1, reach - taker)
    shifted = jax.random.randint(jax.random.fold_in(stream_key, 1), (pairs,), 0, 1 << 20) % (room + 1)
    sizes = sizes.at[1:1 + 2 * pairs:2].set(giver - shifted).at[2:2 + 2 * pairs:2].set(taker + shifted)
    return sizes[jax.random.permutation(jax.random.fold_in(stream_key, 2), number_of)]


def centred(key, dims, scale, most, cuts=(), held_as=jnp.bfloat16):
    array = jax.random.normal(key, dims, jnp.float32) * scale
    if len(cuts) > 0:
        array = levels(key, dims, cuts, -0.22, 0.18) * array
    return jnp.clip(array, min=-most, max=most).astype(held_as)


def setup_inputs(seed: int = 0) -> dict:
    seeds = jax.random.split(jax.random.key(seed), 19)
    return {
        "hidden_in": centred(seeds[0], (TOKENS, D), 1.0, 6.0, ((0, 16),)),
        "gate_proj": centred(seeds[1], (D, DI), D ** -0.5, 0.15625, ((0, 32),), jnp.float32),
        "inner_proj": centred(seeds[2], (D, DI), D ** -0.5, 0.15625, ((0, 32),), jnp.float32),
        "small_proj": centred(seeds[3], (D, 2 * N + H), D ** -0.5, 0.15625, ((0, 32),), jnp.float32),
        "row_layout": jax.random.permutation(seeds[4], BLOCKS).astype(jnp.int32),
        "conv_inner": centred(seeds[5], (CONV, DI), CONV ** -0.5, 3.0, ((1, 2),), jnp.float32),
        "conv_shared": centred(seeds[6], (CONV, 2 * N), CONV ** -0.5, 3.0, (), jnp.float32),
        "bias_inner": centred(seeds[7], (DI,), 0.5, 3.0, ((0, 2),), jnp.float32),
        "bias_shared": centred(seeds[8], (2 * N,), 0.5, 3.0, (), jnp.float32),
        "dt_bias": jnp.clip(-4.0 + 3.0 * jax.random.uniform(seeds[9], (H,), jnp.float32) ** levels(seeds[9], (H,), ((0, 2),), -0.2, 0.2), -4.0, -1.0),
        "decay_log": jnp.clip(-8.0 + 8.0 * jax.random.uniform(seeds[10], (H,), jnp.float32) ** levels(seeds[10], (H,), ((0, 2),), -0.2, 0.2), -8.0, 0.0),
        "skip_gain": jnp.clip(0.5 + 1.5 * jax.random.uniform(seeds[11], (H,), jnp.float32) ** levels(seeds[11], (H,), ((0, 2),), -0.2, 0.2), 0.5, 2.0),
        "norm_gain": jnp.clip(1.0 + 0.18 * jax.random.normal(seeds[12], (DI,), jnp.float32), 0.1, 1.9),
        "out_proj": centred(seeds[13], (DI, D), DI ** -0.5, 0.109375, ((0, 2), (1, 16)), jnp.float32),
        "prompt_lengths": ragged(seeds[14], PROMPTS, TOKENS, MOST, 2).astype(jnp.int32),
        "group_map": set_ends(jax.random.randint(seeds[15], (PROMPTS,), 0, GROUPS), jax.random.fold_in(seeds[15], 1), 0, GROUPS - 1).astype(jnp.int32),
        "init_states": centred(seeds[16], (GROUPS, H, P_SIZE, N), 2.0, 12.0, ((1, 2),), jnp.float32),
        "page_table": draw_page_table(jax.random.fold_in(seeds[18], 71), 0),
    }


epsilon = 1e-05

def token_meta(positions, lengths, groups, group_count):
    starts = jnp.cumsum(lengths) - lengths
    prompt_id = lax.optimization_barrier(jnp.sum((starts[None, :] <= positions[:, None]).astype(jnp.int32), axis=1)) - 1
    prompt_hot = prompt_id[:, None] == jnp.arange(lengths.shape[0], dtype=jnp.int32)[None, :]
    first_pos = lax.optimization_barrier(jnp.sum(jnp.where(prompt_hot, starts[None, :], 0), axis=1))
    group_id = lax.optimization_barrier(jnp.sum(jnp.where(prompt_hot, groups[None, :], 0), axis=1))
    group_hot = (group_id[:, None] == jnp.arange(group_count, dtype=jnp.int32)[None, :]).astype(jnp.float32)
    offset = positions - first_pos
    is_start = (offset == 0).astype(jnp.float32)
    return (prompt_id, offset, is_start, group_hot)

def conv_apply(source, edges, taps, conv_bias, offset):
    padded = jnp.concatenate([edges, source], axis=0).astype(jnp.float32)
    total_rows = source.shape[0]
    width = taps.shape[0]
    result = conv_bias[None, :] + jnp.zeros((total_rows, source.shape[1]), jnp.float32)
    for lag_index in range(width):
        within = (offset >= lag_index).astype(jnp.float32)[:, None]
        lo_row = width - 1 - lag_index
        result = result + taps[lag_index][None, :] * padded[lo_row:lo_row + total_rows] * within
    return jax.nn.silu(result)

def span_terms(x_span, b_span, c_span, dt_span, log_span, pid_span, start_span, group_span, init_states, skip_gain):
    highest = lax.Precision.HIGHEST
    length = x_span.shape[0]
    cumulative = jnp.cumsum(log_span, axis=0)
    before_log = cumulative - log_span
    slots = jnp.arange(length, dtype=jnp.int32)
    causal = (slots[:, None] >= slots[None, :]) & (pid_span[:, None] == pid_span[None, :])
    within = causal[:, :, None]
    decays = jnp.where(within, jnp.exp(jnp.where(within, cumulative[:, None, :] - cumulative[None, :, :], 0.0)), 0.0)
    scores = jnp.dot(c_span, b_span.T, precision=highest)
    mixing = decays * dt_span[None, :, :] * scores[:, :, None]
    y_part = jnp.einsum('tsh,shp->thp', mixing, x_span, precision=highest)
    opening = jnp.where(within, jnp.exp(jnp.where(within, cumulative[:, None, :] - before_log[None, :, :], 0.0)), 0.0)
    opening = lax.optimization_barrier(jnp.sum(opening * start_span[None, :, None], axis=1))
    read_init = jnp.einsum('tn,ghpn->tghp', c_span, init_states, precision=highest)
    read_init = jnp.einsum('tg,tghp->thp', group_span, read_init, precision=highest)
    y_part = y_part + opening[:, :, None] * read_init + skip_gain[None, :, None] * x_span
    weights_last = decays[length - 1] * dt_span
    summary = jnp.einsum('sh,shp,sn->hpn', weights_last, x_span, b_span, precision=highest)
    init_last = jnp.einsum('g,ghpn->hpn', group_span[length - 1], init_states, precision=highest)
    summary = summary + opening[length - 1][:, None, None] * init_last
    alive_mask = (pid_span == pid_span[0]).astype(jnp.float32) * (1.0 - start_span[0])
    carried = alive_mask[:, None] * jnp.exp(cumulative)
    return (y_part, summary, carried[length - 1], carried)

def unpermute(stored, row_layout):
    block_count = row_layout.shape[0]
    block_rows = stored.shape[0] // block_count
    blocks = stored.astype(jnp.bfloat16).reshape(block_count, block_rows, stored.shape[1])
    return jnp.zeros_like(blocks).at[row_layout].set(blocks).reshape(stored.shape)

def reference(hidden_in, gate_proj, inner_proj, small_proj, row_layout, conv_inner, conv_shared, bias_inner, bias_shared, dt_bias, decay_log, skip_gain, norm_gain, out_proj, prompt_lengths, group_map, init_states, page_table):
    highest = lax.Precision.HIGHEST
    gate_val = jnp.dot(hidden_in, unpermute(gate_proj, row_layout), preferred_element_type=jnp.float32).astype(jnp.bfloat16)
    inner_val = jnp.dot(hidden_in, unpermute(inner_proj, row_layout), preferred_element_type=jnp.float32).astype(jnp.bfloat16)
    shared_val = jnp.dot(hidden_in, unpermute(small_proj, row_layout), preferred_element_type=jnp.float32).astype(jnp.bfloat16)
    shared_bc = shared_val[:, :2 * N]
    dt_raw = shared_val[:, 2 * N:]
    positions = jnp.arange(TOKENS, dtype=jnp.int32)
    prompt_id, offset, is_start, group_hot = token_meta(positions, prompt_lengths, group_map, GROUPS)
    x_conv = conv_apply(inner_val, jnp.zeros((CONV - 1, DI), jnp.bfloat16), conv_inner, bias_inner, offset)
    bc_conv = conv_apply(shared_bc, jnp.zeros((CONV - 1, 2 * N), jnp.bfloat16), conv_shared, bias_shared, offset)
    dt_val = jax.nn.softplus(dt_raw.astype(jnp.float32) + dt_bias[None, :])
    log_rate = -jnp.exp(decay_log)[None, :] * dt_val
    spans = TOKENS // PAGE
    items = (x_conv.reshape(spans, PAGE, H, P_SIZE), bc_conv[:, :N].reshape(spans, PAGE, N), bc_conv[:, N:].reshape(spans, PAGE, N), dt_val.reshape(spans, PAGE, H), log_rate.reshape(spans, PAGE, H), prompt_id.reshape(spans, PAGE), is_start.reshape(spans, PAGE), group_hot.reshape(spans, PAGE, GROUPS))

    def advance(running, span_items):
        y_part, summary, decays, carried = span_terms(*span_items, init_states, skip_gain)
        y_part = y_part + carried[:, :, None] * jnp.einsum('tn,hpn->thp', span_items[2], running, precision=highest)
        ending = decays[:, None, None] * running + summary
        return (ending, (y_part, ending))
    _, (y_parts, endings) = lax.scan(advance, jnp.zeros((H, P_SIZE, N), jnp.float32), items)
    state_pages = jnp.zeros_like(endings).at[page_table].set(endings)
    gated = y_parts.reshape(TOKENS, DI) * jax.nn.silu(gate_val.astype(jnp.float32))
    squares = lax.optimization_barrier(jnp.sum(gated * gated, axis=1))
    normed = (gated * lax.rsqrt(squares / DI + epsilon)[:, None] * norm_gain[None, :]).astype(jnp.bfloat16)
    mixed_out = jnp.dot(normed, out_proj.astype(jnp.bfloat16), preferred_element_type=jnp.float32).astype(jnp.bfloat16)
    return (mixed_out, state_pages)
```

```python
import functools

import jax
import jax.numpy as jnp
from jax import lax
from jax.experimental import pallas as pl
from jax.experimental.pallas import tpu as pltpu
from jax.sharding import Mesh
from jax.sharding import PartitionSpec as P

N = 128
CONV = 4
PAGE = 128
HALO = 32
TILE = 16
LANES = 128
EPSILON = 1e-05
F32 = jnp.float32
BF16 = jnp.bfloat16
HIGHEST = lax.Precision.HIGHEST
GROUP = ("a", "b", "tp")
SEQ = ("t", "a", "y", "b")
VMEM = pl.BlockSpec(memory_space=pltpu.VMEM)
SMEM = pl.BlockSpec(memory_space=pltpu.SMEM)


def call(body, name, out_shape, ins, scratch=(), limit=40):
    specs = [SMEM if x.dtype == jnp.int32 else VMEM for x in ins]
    return pl.pallas_call(
        body,
        name=name,
        out_shape=out_shape,
        in_specs=specs,
        out_specs=jax.tree.map(lambda _: VMEM, out_shape),
        scratch_shapes=list(scratch),
        compiler_params=pltpu.CompilerParams(vmem_limit_bytes=limit << 20),
    )(*ins)


def shape(dims, dtype):
    return jax.ShapeDtypeStruct(dims, dtype)


def dot(x, y, dims=((1,), (0,)), precision=None):
    return lax.dot_general(x, y, (dims, ((), ())), precision=precision, preferred_element_type=F32)


NT = ((1,), (1,))
TN = ((0,), (0,))


def swap(x, axis):
    return lax.ppermute(x, axis, [(0, 1), (1, 0)])


def stored_block(s, dy, place, info):
    t, y, count = info[3], info[4], info[5]
    a, b, c = place // 4, (place // 2) % 2, place % 2
    source = lax.rem(t - s + count, count)
    seq = ((source * 2 + a) * 2 + (y ^ dy)) * 2 + b
    return seq * 2 + c


def pieces_of(hidden, info):
    own, mine_b, mine_a, mine_d, other_b, other_a, other_d = hidden
    me, c = info[0], info[1]
    half = own.shape[0] // 2
    yield me * 2, lambda: own[:half]
    yield me * 2 + 1, lambda: own[half:]
    for rel, mine, other in ((1, mine_b, other_b), (2, mine_a, other_a), (3, mine_d, other_d)):
        yield (me ^ rel) * 2 + c, lambda mine=mine: mine[...]
        yield (me ^ rel) * 2 + 1 - c, lambda other=other: other[...]


def inner_kernel(count, rows, *refs):
    info, layout = refs[0], refs[1]
    hidden = refs[2:9]
    parts = refs[9 : 9 + count]
    raw_ref, shared_ref, step_ref, weights = refs[9 + count :]
    width = parts[0].shape[1]
    if rows % TILE == 0 and count > 1:
        lane = lax.broadcasted_iota(jnp.int32, (TILE, LANES), 1) // TILE
        for index in range(count):
            part = parts[index]
            for place in range(8):
                block = layout[stored_block(index // 2, index % 2, place, info)]
                at = pl.multiple_of(block * rows, TILE)
                weights[pl.ds(at, rows), :width] = part[place * rows : (place + 1) * rows, :]
                for piece in range(rows // TILE):
                    packed = part[8 * rows : 8 * rows + TILE, piece * LANES : (piece + 1) * LANES]
                    kept = jnp.where(lane == place, packed, jnp.zeros_like(packed))
                    at2 = pl.multiple_of(block * rows + piece * TILE, TILE)
                    weights[pl.ds(at2, TILE), width:] = kept
        w = weights
    else:
        w = parts[0]
    bc = raw_ref.shape[2]
    for index, rows_of in pieces_of(hidden, info):
        result = dot(rows_of(), w[...])
        raw_ref[index] = result[:, :bc].astype(BF16)
        shared_ref[index] = result[:, bc : bc + LANES].astype(BF16)
        step = result[:, bc + LANES :]
        for shift in (64, 32, 16):
            step = step + pltpu.roll(step, shift, 1)
        step_ref[index] = step


def gate_kernel(count, rows, *refs):
    info, layout = refs[0], refs[1]
    hidden = refs[2:9]
    parts = refs[9 : 9 + count]
    gate_ref, weights = refs[9 + count :]
    if rows % TILE == 0 and count > 1:
        for index in range(count):
            for place in range(8):
                block = layout[stored_block(index // 2, index % 2, place, info)]
                at = pl.multiple_of(block * rows, TILE)
                weights[pl.ds(at, rows), :] = parts[index][place * rows : (place + 1) * rows, :]
        w = weights
    else:
        w = parts[0]
    for index, rows_of in pieces_of(hidden, info):
        result = dot(rows_of(), w[...])
        gate_ref[index] = jax.nn.silu(result).astype(BF16)


def chunk_start(i, info, tokens):
    t, y = info[3], info[4]
    per = tokens // PAGE
    q = i // per
    seq = ((t * 2 + q // 2) * 2 + y) * 2 + q % 2
    return seq * tokens + (i % per) * PAGE


def last_start(position, starts):
    best = jnp.int32(0)
    for k in range(starts.shape[0]):
        best = jnp.maximum(best, jnp.where(starts[k] <= position, starts[k], 0))
    return best


def first_positions(first, starts, dims):
    position = first + lax.broadcasted_iota(jnp.int32, dims, 0)
    best = jnp.zeros(dims, jnp.int32)
    for k in range(starts.shape[0]):
        best = jnp.maximum(best, jnp.where(starts[k] <= position, starts[k], 0))
    return best


def conv_silu(window, taps, bias, offset):
    total = bias + taps[0:1, :] * window[TILE : TILE + PAGE]
    for lag in range(1, CONV):
        within = (offset >= lag).astype(F32)
        total = total + taps[lag : lag + 1, :] * window[TILE - lag : TILE - lag + PAGE] * within
    return total / (1.0 + jnp.exp(-total))


def pair_columns(values, pair):
    lane = lax.broadcasted_iota(jnp.int32, (PAGE, LANES), 1)
    left = values[:, 2 * pair : 2 * pair + 1]
    right = values[:, 2 * pair + 1 : 2 * pair + 2]
    return jnp.where(lane < 64, left, right)


def state_kernel(heads, tokens, info, starts, groups, raw, own, other, step, taps, bias, taps2,
                 bias2, dt_bias, decay, init, x_ref, b_ref, c_ref, cum_ref, dt_ref, end_ref,
                 factor_ref, summary_ref, state, factor):
    chunks = x_ref.shape[0]
    per_run = chunks // 2
    per = tokens // PAGE
    pairs = heads // 2
    rate = -jnp.exp(decay[...])
    row = lax.broadcasted_iota(jnp.int32, (PAGE, PAGE), 0)
    col = lax.broadcasted_iota(jnp.int32, (PAGE, PAGE), 1)
    below = (row >= col).astype(F32)

    def one(i, carry):
        @pl.when(i % per_run == 0)
        def _():
            state[...] = jnp.zeros_like(state)
            factor[...] = jnp.ones_like(factor)

        first = chunk_start(i, info, tokens)
        opened = last_start(first + PAGE - 1, starts)
        alive = (opened < first).astype(F32)
        start_of = first_positions(first, starts, (PAGE, 1))
        offset = first + lax.broadcasted_iota(jnp.int32, (PAGE, 1), 0) - start_of
        q = i // per
        at = pl.multiple_of(HALO - TILE + (i % per) * PAGE, TILE)
        window = pl.ds(at, PAGE + TILE)
        x = conv_silu(raw[q, window, :].astype(F32), taps, bias[...], offset)
        is_first = info[1] == 0
        mine, theirs = own[q, window, :].astype(F32), other[q, window, :].astype(F32)
        b_raw = jnp.where(is_first, mine, theirs)
        c_raw = jnp.where(is_first, theirs, mine)
        b = conv_silu(b_raw, taps2[:, :LANES], bias2[:, :LANES], offset).astype(BF16)
        c = conv_silu(c_raw, taps2[:, LANES:], bias2[:, LANES:], offset).astype(BF16)
        raw_step = step[q, pl.ds(pl.multiple_of(HALO + (i % per) * PAGE, TILE), PAGE), :]
        v = raw_step + dt_bias[...]
        dt = jnp.maximum(v, 0.0) + jnp.log1p(jnp.exp(-jnp.abs(v)))
        log_rate = rate * dt
        cum = dot(below, log_rate, precision=HIGHEST)
        last = cum[PAGE - 1 : PAGE, :]
        kept = (row >= opened - first).astype(F32)
        weight = jnp.exp(last - cum) * dt * kept
        cum_t = cum.T
        x_ref[i] = x.astype(BF16)
        b_ref[i] = b
        c_ref[i] = c
        cum_ref[i] = cum
        dt_ref[i] = dt
        whole = jnp.broadcast_to(jnp.exp(cum_t[0:8, PAGE - 1 : PAGE]), (8, LANES)) * alive
        for pair in range(pairs):
            scaled = (x[:, pair * LANES : (pair + 1) * LANES] * pair_columns(weight, pair)).astype(BF16)
            added = dot(scaled, b, TN)
            for k in (0, 1):
                h = 2 * pair + k
                here = slice(h * 64, (h + 1) * 64)
                state[here, :] = state[here, :] * whole[h : h + 1, :] + added[k * 64 : (k + 1) * 64, :]
        for k in range(starts.shape[0]):
            start = starts[k]

            @pl.when((start >= first) & (start == opened))
            def _():
                before = jnp.sum(jnp.where(col == start - first - 1, cum_t, 0.0), axis=1, keepdims=True)
                opening = jnp.exp(cum_t[0:8, PAGE - 1 : PAGE] - before[0:8])
                opening = jnp.broadcast_to(opening, (8, LANES))
                for h in range(heads):
                    here = slice(h * 64, (h + 1) * 64)
                    state[here, :] = state[here, :] + opening[h : h + 1, :] * init[groups[k], here, :]

        factor[...] = factor[...] * whole
        end_ref[i] = state[...]
        factor_ref[i] = factor[...]

        @pl.when(i % per_run == per_run - 1)
        def _():
            summary_ref[i // per_run, : heads * 64, :] = state[...].astype(BF16)
            tail = jnp.concatenate([factor[...], jnp.zeros_like(factor[...])], axis=0)
            summary_ref[i // per_run, heads * 64 :, :] = tail.astype(BF16)

        return carry

    lax.fori_loop(0, chunks, one, 0)


def within_kernel(heads, tokens, info, starts, groups, x_ref, b_ref, c_ref, cum_ref, dt_ref, skip,
                  init, y_ref):
    chunks = x_ref.shape[0]
    pairs = heads // 2
    row = lax.broadcasted_iota(jnp.int32, (PAGE, PAGE), 0)
    col = lax.broadcasted_iota(jnp.int32, (PAGE, PAGE), 1)
    lane = lax.broadcasted_iota(jnp.int32, (PAGE, LANES), 1)

    def one(i, carry):
        first = chunk_start(i, info, tokens)
        start_of = first_positions(first, starts, (PAGE, PAGE))
        bias = jnp.where((row >= col) & (col >= start_of - first), 0.0, -1e30)
        b, c = b_ref[i], c_ref[i]
        cum, dt = cum_ref[i], dt_ref[i]
        cum_t = cum.T
        scores = dot(c, b, NT)
        for pair in range(pairs):
            here = slice(pair * LANES, (pair + 1) * LANES)
            x = x_ref[i, :, here].astype(F32)
            scaled = x * pair_columns(dt, pair)
            mixing = []
            for h in (2 * pair, 2 * pair + 1):
                gap = cum[:, h : h + 1] + bias - cum_t[h : h + 1, :]
                mixing.append((scores * jnp.exp(gap)).astype(BF16))
            both = jnp.concatenate(
                [jnp.where(lane < 64, scaled, 0.0), jnp.where(lane < 64, 0.0, scaled)], axis=0
            ).astype(BF16)
            y = dot(jnp.concatenate(mixing, axis=1), both)
            y_ref[i, :, here] = y + skip[:, here] * x
        for k in range(starts.shape[0]):
            start = starts[k]

            @pl.when((start >= first) & (start < first + PAGE))
            def _():
                before = jnp.sum(jnp.where(row == start - first - 1, cum, 0.0), axis=0, keepdims=True)
                opening = jnp.exp(jnp.minimum(cum - before, 0.0))
                opening = jnp.where(start_of == start, opening, 0.0)
                for pair in range(pairs):
                    here = slice(pair * LANES, (pair + 1) * LANES)
                    read = dot(c, init[groups[k], here, :].astype(BF16), NT)
                    y_ref[i, :, here] = y_ref[i, :, here] + pair_columns(opening, pair) * read

        return carry

    lax.fori_loop(0, chunks, one, 0)


def onto(run, h, before):
    here = slice(h * 64, (h + 1) * 64)
    decay = run[run.shape[0] - 16 + h : run.shape[0] - 16 + h + 1, :].astype(F32)
    return decay * before + run[here, :].astype(F32)


def compose_kernel(heads, info, mine, theirs, block_ref):
    low = info[4] == 0
    runs = []
    for a in range(2):
        m, q = mine[a].astype(F32), theirs[a].astype(F32)
        runs += [jnp.where(low, m, q), jnp.where(low, q, m)]
    total = runs[0]
    for run in runs[1:]:
        parts = []
        for h in range(heads):
            parts.append(onto(run, h, total[h * 64 : (h + 1) * 64, :]))
        tail = total[heads * 64 :, :] * run[heads * 64 :, :]
        total = jnp.concatenate(parts + [tail], axis=0)
    block_ref[...] = total.astype(BF16)


def finish_kernel(heads, tokens, info, starts, mine, theirs, entering, c_ref, cum_ref, end_ref,
                  factor_ref, y_ref, gate, gain, mixed_ref, square_ref, page_ref, starting, state):
    chunks = c_ref.shape[0]
    per = tokens // PAGE
    per_run = chunks // 2
    pairs = heads // 2
    me, y = info[0], info[4]
    for h in range(heads):
        here = slice(h * 64, (h + 1) * 64)
        outside = entering[here, :].astype(F32)
        first = jnp.where(y == 0, outside, onto(theirs[0], h, outside))
        starting[0, here, :] = first
        second = onto(mine[0], h, first)
        third = jnp.where(y == 0, onto(theirs[0], h, second), onto(theirs[1], h, second))
        starting[1, here, :] = third
    ones = jnp.ones((8, LANES), F32)

    def one(i, carry):
        run = i // per_run

        @pl.when(i % per_run == 0)
        def _():
            state[...] = starting[run]

        q = i // per
        first = chunk_start(i, info, tokens)
        alive = (first_positions(first, starts, (PAGE, LANES)) < first).astype(F32)
        decay = jnp.exp(cum_ref[i]) * alive
        read = dot(c_ref[i], state[...].astype(BF16), NT)
        rows = pl.ds(pl.multiple_of(HALO + (i % per) * PAGE, TILE), PAGE)
        squares = jnp.zeros((PAGE, LANES), F32)
        for pair in range(pairs):
            here = slice(pair * LANES, (pair + 1) * LANES)
            value = y_ref[i, :, here] + pair_columns(decay, pair) * read[:, here]
            value = value * gate[q, rows, here].astype(F32)
            mixed_ref[i, :, here] = (value * gain[:, here]).astype(BF16)
            squares = squares + value * value
        square_ref[i] = dot(ones, squares, NT, HIGHEST)
        for h in range(heads):
            here = slice(h * 64, (h + 1) * 64)
            after = end_ref[i, here, :] + factor_ref[i, h : h + 1, :] * starting[run, here, :]
            state[here, :] = after
        page_ref[q ^ me, i % per] = state[...].astype(BF16)
        return carry

    lax.fori_loop(0, chunks, one, 0)


def columns_kernel(count, rows, *refs):
    info = refs[0]
    parts = refs[1 : 1 + count]
    out = refs[1 + count]
    for index in range(count):
        for place in range(4):
            seq = stored_block(index // 2, index % 2, 2 * place, info) // 2
            at = pl.multiple_of(seq * rows, TILE)
            out[pl.ds(at, rows), :] = parts[index][place * rows : (place + 1) * rows, :]


def mix_kernel(keep, info, mixed, columns, out):
    me, c = info[0], info[1]
    half = c if keep else 1 - c
    for rel in range(4):
        out[rel] = dot(mixed[(me ^ rel) * 2 + half], columns[...], NT).astype(BF16)


def page_kernel(info, table, own, from_b, from_a, from_d, out):
    me, seq, per = info[0], info[6], own.shape[0]
    for k in range(per):
        slot = table[k] - seq * per
        for rel, source in enumerate((own, from_b, from_a, from_d)):
            out[slot, me ^ rel] = source[k].astype(F32)


def weight_parts(part, count):
    parts = []
    for s in range(count):
        if s > 0:
            part = lax.ppermute(part, "t", [(i, (i + 1) % count) for i in range(count)])
        parts += [part, swap(part, "y")]
    return parts


def in_order(parts, index):
    stacked = jnp.stack(parts)
    blocks = stacked.reshape((-1, stacked.shape[1] * len(parts) // index.shape[0], stacked.shape[2]))
    return jnp.zeros_like(blocks).at[index].set(blocks).reshape(-1, stacked.shape[2])


def on_device(
    hidden_in,
    gate_proj,
    inner_proj,
    small_proj,
    row_layout,
    conv_inner,
    conv_shared,
    bias_inner,
    bias_shared,
    dt_bias,
    decay_log,
    skip_gain,
    norm_gain,
    out_proj,
    prompt_lengths,
    group_map,
    init_states,
    page_table,
):
    tokens, model = hidden_in.shape
    rows = gate_proj.shape[0]
    half_heads = dt_bias.shape[0]
    heads = half_heads // 4
    inner = conv_inner.shape[1]
    head_dim = inner // half_heads
    width = heads * head_dim
    t_count = lax.axis_size("t")
    t, a, y, b, c = (lax.axis_index(name) for name in ("t", "a", "y", "b", "tp"))
    me = a * 2 + b
    seq = ((t * 2 + a) * 2 + y) * 2 + b
    info = jnp.stack([me, c, 0 * c, t, y, 0 * c + t_count, seq, 0 * c]).astype(jnp.int32)
    starts = (jnp.cumsum(prompt_lengths) - prompt_lengths).astype(jnp.int32)
    count = 2 * t_count

    inner_send = inner_proj.astype(BF16).reshape(rows, 2, 4, width).transpose(2, 1, 0, 3)
    small = small_proj.astype(BF16)
    shared_send = small[:, : 2 * N].reshape(rows, 2, N).transpose(1, 0, 2)
    shared_send = jnp.broadcast_to(shared_send[None], (4, 2, rows, N))
    step_send = small[:, 2 * N :].reshape(rows, 2, 4, heads).transpose(2, 1, 0, 3)
    step_send = jnp.pad(step_send, ((0, 0), (0, 0), (0, 0), (0, LANES - heads)))
    inner_send = jnp.concatenate([inner_send, shared_send, step_send], axis=-1)
    inner_send = inner_send.reshape(8, rows, width + N + LANES)
    inner_got = lax.all_to_all(inner_send, GROUP, 0, 0, tiled=True)
    gate_send = gate_proj.astype(BF16).reshape(rows, 2, 4, width).transpose(2, 1, 0, 3)
    gate_got = lax.all_to_all(gate_send.reshape(8, rows, width), GROUP, 0, 0, tiled=True)
    out_send = out_proj.T.astype(BF16).reshape(out_proj.shape[1], 4, width).transpose(1, 0, 2)
    out_got = lax.all_to_all(out_send, ("a", "b"), 0, 0, tiled=True)

    wide = width + N + LANES
    if rows % TILE == 0:
        packed = inner_got[:, :, width + N : width + N + 16].reshape(8, rows // TILE, TILE, 16)
        packed = packed.transpose(2, 1, 0, 3).reshape(TILE, rows // TILE * LANES)
        packed = jnp.pad(packed, ((0, 0), (0, width + N - packed.shape[1])))
        inner_part = jnp.concatenate([inner_got[:, :, : width + N].reshape(8 * rows, -1), packed])
    else:
        inner_part = inner_got.reshape(8 * rows, wide)
    inner_parts = weight_parts(inner_part, t_count)
    gate_parts = weight_parts(gate_got.reshape(8 * rows, width), t_count)
    out_rows = out_proj.shape[1]
    out_parts = weight_parts(out_got.reshape(4 * out_rows, width), t_count)
    if rows % TILE != 0:
        index = [stored_block(s, dy, p, info) for s in range(t_count) for dy in (0, 1) for p in range(8)]
        index = row_layout[jnp.stack(index)]
        inner_parts = [in_order(inner_parts, index)]
        gate_parts = [in_order(gate_parts, index)]
    if out_rows % TILE != 0:
        index = [
            stored_block(s, dy, 2 * p, info) // 2
            for s in range(t_count)
            for dy in (0, 1)
            for p in range(4)
        ]
        columns = in_order(out_parts, jnp.stack(index))
    else:
        columns = call(
            functools.partial(columns_kernel, count, out_rows),
            "columns",
            shape((model, width), BF16),
            [info, *out_parts],
        )

    size = lax.axis_size(SEQ)
    halo = lax.ppermute(hidden_in[tokens - HALO :], SEQ, [(i, i + 1) for i in range(size - 1)])
    own = jnp.concatenate([halo, hidden_in], axis=0)
    half = own.shape[0] // 2
    mine = lax.dynamic_slice_in_dim(own, c * half, half, 0)
    mine_b, mine_a = swap(mine, "b"), swap(mine, "a")
    cut = -(-half // (2 * TILE)) * TILE
    mine_d = jnp.concatenate([swap(mine_a[:cut], "b"), swap(mine_b[cut:], "a")], axis=0)
    hidden = [own, mine_b, mine_a, mine_d, swap(mine_b, "tp"), swap(mine_a, "tp"), swap(mine_d, "tp")]

    raw, shared, step = call(
        functools.partial(inner_kernel, len(inner_parts), rows),
        "inner_projection",
        (
            shape((8, half, width), BF16),
            shape((8, half, LANES), BF16),
            shape((8, half, LANES), F32),
        ),
        [info, row_layout, *hidden, *inner_parts],
        [pltpu.VMEM((model, wide), BF16)],
    )
    shared_other = swap(shared, "tp")
    gate = call(
        functools.partial(gate_kernel, len(gate_parts), rows),
        "gate_projection",
        shape((8, half, width), BF16),
        [info, row_layout, *hidden, *gate_parts],
        [pltpu.VMEM((model, width), BF16)],
    )

    def whole(x):
        return x.reshape(4, 2 * half, x.shape[2])

    def lanes_of(x):
        mine = lax.dynamic_slice_in_dim(x, me * heads, heads, 0)
        return jnp.pad(mine, (0, LANES - heads))[None]

    taps = lax.dynamic_slice_in_dim(conv_inner, me * width, width, 1)
    bias = lax.dynamic_slice_in_dim(bias_inner, me * width, width, 0)[None]
    gain = lax.dynamic_slice_in_dim(norm_gain, me * width, width, 0)[None]
    skip = jnp.repeat(lax.dynamic_slice_in_dim(skip_gain, me * heads, heads, 0), head_dim)[None]
    init = lax.dynamic_slice_in_dim(init_states, me * heads, heads, 1)
    init = init.reshape(init.shape[0], width, N)
    chunks = 4 * tokens // PAGE
    x, b_in, c_in, cum, dt, ends, factors, summary = call(
        functools.partial(state_kernel, heads, tokens),
        "states",
        (
            shape((chunks, PAGE, width), BF16),
            shape((chunks, PAGE, N), BF16),
            shape((chunks, PAGE, N), BF16),
            shape((chunks, PAGE, LANES), F32),
            shape((chunks, PAGE, LANES), F32),
            shape((chunks, width, N), F32),
            shape((chunks, 8, N), F32),
            shape((2, width + 16, N), BF16),
        ),
        [info, starts, group_map, whole(raw), whole(shared), whole(shared_other), whole(step), taps,
         bias, conv_shared, bias_shared[None], lanes_of(dt_bias), lanes_of(decay_log), init],
        [pltpu.VMEM((width, N), F32), pltpu.VMEM((8, N), F32)],
    )
    theirs = swap(summary, "y")
    block = call(
        functools.partial(compose_kernel, heads),
        "compose",
        shape((width + 16, N), BF16),
        [info, summary, theirs],
    )
    onward = [(i, i + 1) for i in range(t_count - 1)]
    block = lax.ppermute(block, "t", onward)
    entering = block[:width]
    if t_count > 2:
        total = entering.astype(F32).reshape(heads, head_dim, N)
        decay = block[width : width + heads, None, :].astype(F32)
        for _ in range(t_count - 2):
            block = lax.ppermute(block, "t", onward)
            total = total + decay * block[:width].astype(F32).reshape(heads, head_dim, N)
            decay = decay * block[width : width + heads, None, :].astype(F32)
        entering = total.reshape(width, N)
    y_within = call(
        functools.partial(within_kernel, heads, tokens),
        "within_chunks",
        shape((chunks, PAGE, width), F32),
        [info, starts, group_map, x, b_in, c_in, cum, dt, skip, init],
    )
    mixed, squares, pages = call(
        functools.partial(finish_kernel, heads, tokens),
        "finish",
        (
            shape((chunks, PAGE, width), BF16),
            shape((chunks, 8, PAGE), F32),
            shape((4, tokens // PAGE, width, N), BF16),
        ),
        [info, starts, summary, theirs, entering, c_in, cum, ends, factors, y_within, whole(gate), gain],
        [pltpu.VMEM((2, width, N), F32), pltpu.VMEM((width, N), F32)],
    )

    across = [(i, i ^ 3) for i in range(4)]
    got = [pages[0], swap(pages[1], "b"), swap(pages[2], "a"), lax.ppermute(pages[3], ("a", "b"), across)]
    per = tokens // PAGE
    state_pages = call(
        page_kernel, "pages", shape((per, 4, width, N), F32), [info, page_table, *got]
    ).reshape(per, half_heads, head_dim, N)

    sent = call(functools.partial(mix_kernel, False), "mix_send", shape((4, PAGE, model), BF16),
                [info, mixed, columns])
    sent = swap(sent, "tp")
    kept = call(functools.partial(mix_kernel, True), "mix_keep", shape((4, PAGE, model), BF16),
                [info, mixed, columns])
    squares = lax.psum(squares[:, 0, :], GROUP)
    mid = model // 2
    total = kept.astype(F32) + sent.astype(F32)
    left, right = total[..., :mid], total[..., mid:]
    left_in = swap(jnp.stack([left[1], left[3]]).astype(BF16), "b")
    right_in = swap(right[2:4].astype(BF16), "a")
    left = jnp.stack([left[0], left[2]]) + left_in.astype(F32)
    right = right[0:2] + right_in.astype(F32)
    left_in = swap(left[1].astype(BF16), "a")
    right_in = swap(right[1].astype(BF16), "b")
    left = left[0] + left_in.astype(F32)
    right = right[0] + right_in.astype(F32)
    mine_squares = lax.dynamic_index_in_dim(squares, me * 2 + c, 0, keepdims=False)
    scale = lax.rsqrt(mine_squares / (2 * inner) + EPSILON)[:, None]
    mixed_out = (jnp.concatenate([left, right], axis=1) * scale).astype(BF16)
    return (mixed_out, state_pages)


def solution(mesh):
    count = mesh.shape["seq"]
    fine = Mesh(mesh.devices.reshape(count // 8, 2, 2, 2, 2), SEQ + ("tp",))
    placed = (
        P(SEQ, None),
        P(SEQ + ("tp",), None),
        P(SEQ + ("tp",), None),
        P(SEQ + ("tp",), None),
        P(),
        P(None, "tp"),
        P(),
        P("tp"),
        P(),
        P("tp"),
        P("tp"),
        P("tp"),
        P("tp"),
        P("tp", SEQ),
        P(),
        P(),
        P(None, "tp", None, None),
        P(SEQ),
    )
    return jax.shard_map(
        on_device,
        mesh=fine,
        in_specs=placed,
        out_specs=(P(SEQ + ("tp",), None), P(SEQ, "tp", None, None)),
        check_vma=False,
    )
```

```python
import functools

import jax
import jax.numpy as jnp
from jax import lax
from jax.experimental import pallas as pl
from jax.experimental.pallas import tpu as pltpu
from jax.sharding import Mesh
from jax.sharding import PartitionSpec as P

N = 128
CONV = 4
PAGE = 128
TILE = 16
LANES = 128
EPSILON = 1e-05
F32 = jnp.float32
BF16 = jnp.bfloat16
HIGHEST = lax.Precision.HIGHEST
GROUP = ("a", "b", "tp")
SEQ = ("t", "a", "y", "b")
VMEM = pl.BlockSpec(memory_space=pltpu.VMEM)
SMEM = pl.BlockSpec(memory_space=pltpu.SMEM)


def call(body, name, out_shape, ins, scratch=(), after=(), us=1.0, limit=40):
    specs = [SMEM if x.dtype == jnp.int32 else VMEM for x in ins]
    specs += [pl.BlockSpec(memory_space=pl.ANY)] * len(after)
    first, last = len(ins), len(ins) + len(after)

    def kernel(*refs):
        body(*refs[:first], *refs[last:])

    return pl.pallas_call(
        kernel,
        name=name,
        out_shape=out_shape,
        in_specs=specs,
        out_specs=jax.tree.map(lambda _: VMEM, out_shape),
        scratch_shapes=list(scratch),
        cost_estimate=pl.CostEstimate(
            flops=int(us * 1e9), bytes_accessed=int(us * 3e6), transcendentals=0
        ),
        compiler_params=pltpu.CompilerParams(vmem_limit_bytes=limit << 20),
    )(*ins, *after)


def shape(dims, dtype):
    return jax.ShapeDtypeStruct(dims, dtype)


def dot(x, y, dims=((1,), (0,)), precision=None):
    return lax.dot_general(x, y, (dims, ((), ())), precision=precision, preferred_element_type=F32)


NT = ((1,), (1,))
TN = ((0,), (0,))


def swap(x, axis):
    return lax.ppermute(x, axis, [(0, 1), (1, 0)])


class Ints:
    def __init__(self, ref, at, size):
        self.ref, self.at, self.size = ref, at, size

    def __getitem__(self, k):
        return self.ref[self.at + k]


def views(ref, sizes):
    out, at = [], 0
    for size in sizes:
        out.append(Ints(ref, at, size))
        at += size
    return out


def stored_block(s, dy, place, info):
    t, y, count = info[3], info[4], info[5]
    a, b, c = place // 4, (place // 2) % 2, place % 2
    source = lax.rem(t - s + count, count)
    seq = ((source * 2 + a) * 2 + (y ^ dy)) * 2 + b
    return seq * 2 + c


def pack_kernel(heads, inner, small, gate, out):
    width = heads * 64
    rows = inner.shape[0]
    lane = lax.broadcasted_iota(jnp.int32, (rows, LANES), 1)
    steps = small[:, 2 * N :]
    steps = jnp.concatenate([steps, jnp.zeros((rows, LANES - steps.shape[1]), F32)], axis=1)
    for place in range(8):
        group, c = place // 2, place % 2
        at = (c * 4 + group) * width
        out[place, :, :width] = inner[:, at : at + width].astype(BF16)
        out[place, :, width : width + N] = small[:, c * N : (c + 1) * N].astype(BF16)
        first = (c * 4 + group) * heads
        moved = pltpu.roll(steps, LANES - first, 1) if first else steps
        out[place, :, width + N : width + N + LANES] = jnp.where(lane < heads, moved, 0.0).astype(BF16)
        out[place, :, width + N + LANES :] = gate[:, at : at + width].astype(BF16)


def repack_kernel(got, whole, low, high, gate):
    rows, width = got.shape[1], whole.shape[1]
    for place in range(8):
        gate[place * rows : (place + 1) * rows, :] = got[place, :, width + LANES :]
    lane = lax.broadcasted_iota(jnp.int32, (TILE, LANES), 1) // TILE
    for place in range(8):
        block = got[place, :, :width]
        whole[place * rows : (place + 1) * rows, :] = block
        half, at = (low, place) if place < 4 else (high, place - 4)
        half[at * rows : (at + 1) * rows, :] = block
    for piece in range(rows // TILE):
        packed = jnp.zeros((TILE, LANES), F32)
        for place in range(8):
            steps = got[place, piece * TILE : (piece + 1) * TILE, width : width + LANES].astype(F32)
            steps = pltpu.roll(steps, place * TILE, 1) if place else steps
            packed = jnp.where(lane == place, steps, packed)
        here = slice(piece * LANES, (piece + 1) * LANES)
        whole[8 * rows :, here] = packed.astype(BF16)
        high[4 * rows :, here] = packed.astype(BF16)
    rest = rows // TILE * LANES
    if rest < width:
        blank = jnp.zeros((TILE, width - rest), BF16)
        whole[8 * rows :, rest:] = blank
        high[4 * rows :, rest:] = blank


def copy_kernel(source, out):
    out[...] = source[...]


def pack_out_kernel(source, out):
    width = out.shape[2]
    for place in range(4):
        out[place] = source[:, place * width : (place + 1) * width].astype(BF16)


def forward_kernel(sizes, ints, mine_b, mine_a, halo0, halo1, over_b, over_a):
    info = views(ints, sizes)[0]
    cut = over_b.shape[0]
    over_b[...] = mine_a[:cut, :]
    over_a[:cut, :] = mine_b[cut:, :]

    @pl.when(info[0] % 2 == 0)
    def _():
        over_a[cut:, :] = halo0[...]

    @pl.when(info[0] % 2 == 1)
    def _():
        over_a[cut:, :] = halo1[...]


def assemble_kernel(sizes, ints, own, mine_b, mine_a, mine_d0, mine_d1, other_b, other_a, other_d0,
                    other_d1, halo0, halo1, out):
    info = views(ints, sizes)[0]
    me, c = info[0], info[1]
    half = own.shape[0] // 2

    def put(q, h, row, source):
        at = TILE + ((q % 2) * 2 + h) * half + row
        out[q // 2, pl.ds(pl.multiple_of(at, TILE), source.shape[0]), :] = source

    put(me, 0, 0, own[:half, :])
    put(me, 1, 0, own[half:, :])
    for h, parts in ((c, (mine_b, mine_a, mine_d0, mine_d1)), (1 - c, (other_b, other_a, other_d0, other_d1))):
        cut = parts[2].shape[0]
        put(me ^ 1, h, 0, parts[0][...])
        put(me ^ 2, h, 0, parts[1][...])
        put(me ^ 3, h, 0, parts[2][...])
        put(me ^ 3, h, cut, parts[3][:cut, :])
    a = me // 2
    out[1 - a, :TILE, :] = mine_d1[cut:, :]

    @pl.when(me % 2 == 0)
    def _():
        out[a, :TILE, :] = halo0[...]

    @pl.when(me % 2 == 1)
    def _():
        out[a, :TILE, :] = halo1[...]


def place_parts(weights, marks, rows, parts, info, layout):
    width = parts[0].shape[1]
    lane = lax.broadcasted_iota(jnp.int32, (TILE, LANES), 1) // TILE
    for (s, dy, first), part in zip(marks, parts):
        count = part.shape[0] // rows
        for k in range(count):
            block = layout[stored_block(s, dy, first + k, info)]
            at = pl.multiple_of(block * rows, TILE)
            weights[pl.ds(at, rows), :width] = part[k * rows : (k + 1) * rows, :]
        base = count * rows
        if part.shape[0] == base:
            continue
        for place in range(8):
            block = layout[stored_block(s, dy, place, info)]
            for piece in range(rows // TILE):
                packed = part[base : base + TILE, piece * LANES : (piece + 1) * LANES]
                kept = jnp.where(lane == place, packed, jnp.zeros_like(packed))
                at = pl.multiple_of(block * rows + piece * TILE, TILE)
                weights[pl.ds(at, TILE), width:] = kept


def inner_kernel(sizes, marks, rows, *refs):
    info, layout = views(refs[0], sizes)[:2]
    hidden = refs[1]
    if marks:
        parts = refs[2 : 2 + len(marks)]
        raw_ref, shared_ref, step_ref, weights = refs[2 + len(marks) :]
        place_parts(weights, marks, rows, parts, info, layout)
    else:
        weights, raw_ref, shared_ref, step_ref = refs[2:6]
    bc = raw_ref.shape[2]
    for run in range(2):
        result = dot(hidden[run], weights[:, bc:])
        shared_ref[run] = result[:, :LANES].astype(BF16)
        step = result[:, LANES:]
        for shift in (64, 32, 16):
            step = step + pltpu.roll(step, shift, 1)
        step_ref[run] = step
        raw_ref[run] = dot(hidden[run], weights[:, :bc]).astype(BF16)


def gate_kernel(sizes, marks, rows, *refs):
    info, layout = views(refs[0], sizes)[:2]
    hidden = refs[1]
    if marks:
        gate_ref, weights = refs[2 + len(marks) :]
        place_parts(weights, marks, rows, refs[2 : 2 + len(marks)], info, layout)
    else:
        weights, gate_ref = refs[2:4]
    for run in range(2):
        gate_ref[run] = jax.nn.silu(dot(hidden[run], weights[...])).astype(BF16)


def starts_of(lengths):
    starts, total = [], jnp.int32(0)
    for k in range(lengths.size):
        starts.append(total)
        total = total + lengths[k]
    return starts


def head_lanes(row, heads, info):
    return pltpu.roll(row, lax.rem(LANES - info[0] * heads, LANES), 1)


def chunk_start(i, info, tokens):
    t, y = info[3], info[4]
    per = tokens // PAGE
    q = i // per
    seq = ((t * 2 + q // 2) * 2 + y) * 2 + q % 2
    return seq * tokens + (i % per) * PAGE


def last_start(position, starts):
    best = jnp.int32(0)
    for k in range(len(starts)):
        best = jnp.maximum(best, jnp.where(starts[k] <= position, starts[k], 0))
    return best


def first_positions(first, starts, dims):
    position = first + lax.broadcasted_iota(jnp.int32, dims, 0)
    best = jnp.zeros(dims, jnp.int32)
    for k in range(len(starts)):
        best = jnp.maximum(best, jnp.where(starts[k] <= position, starts[k], 0))
    return best


def conv_silu(window, taps, bias, offset):
    total = bias + taps[0:1, :] * window[TILE : TILE + PAGE]
    for lag in range(1, CONV):
        within = (offset >= lag).astype(F32)
        total = total + taps[lag : lag + 1, :] * window[TILE - lag : TILE - lag + PAGE] * within
    return total / (1.0 + jnp.exp(-total))


def pair_columns(values, pair):
    lane = lax.broadcasted_iota(jnp.int32, (PAGE, LANES), 1)
    left = values[:, 2 * pair : 2 * pair + 1]
    right = values[:, 2 * pair + 1 : 2 * pair + 2]
    return jnp.where(lane < 64, left, right)


def state_kernel(heads, tokens, sizes, ints, raw, own, other, step, params, init, x_ref, b_ref, c_ref,
                 cum_ref, dt_ref, end_ref, factor_ref, summary_ref, state, factor):
    info, _, lengths, groups = views(ints, sizes)[:4]
    starts = starts_of(lengths)
    width = heads * 64
    here = pl.ds(pl.multiple_of(info[0] * width, LANES), width)
    taps, bias = params[0:4, here], params[4:5, here]
    taps2, bias2 = params[8:12, : 2 * N], params[12:13, : 2 * N]
    per_head = head_lanes(params[8:16, 2 * N : 2 * N + LANES], heads, info)
    dt_bias, rate = per_head[0:1], -jnp.exp(per_head[1:2])
    chunks = x_ref.shape[0]
    per_run = chunks // 2
    pairs = heads // 2
    row = lax.broadcasted_iota(jnp.int32, (PAGE, PAGE), 0)
    col = lax.broadcasted_iota(jnp.int32, (PAGE, PAGE), 1)
    below = (row >= col).astype(F32)

    def one(i, carry):
        @pl.when(i % per_run == 0)
        def _():
            state[...] = jnp.zeros_like(state)
            factor[...] = jnp.ones_like(factor)

        first = chunk_start(i, info, tokens)
        opened = last_start(first + PAGE - 1, starts)
        alive = (opened < first).astype(F32)
        start_of = first_positions(first, starts, (PAGE, 1))
        offset = first + lax.broadcasted_iota(jnp.int32, (PAGE, 1), 0) - start_of
        q = i // per_run
        at = pl.multiple_of((i % per_run) * PAGE, TILE)
        window = pl.ds(at, PAGE + TILE)
        x = conv_silu(raw[q, window, :].astype(F32), taps, bias, offset)
        is_first = info[1] == 0
        mine, theirs = own[q, window, :].astype(F32), other[q, window, :].astype(F32)
        b_raw = jnp.where(is_first, mine, theirs)
        c_raw = jnp.where(is_first, theirs, mine)
        b = conv_silu(b_raw, taps2[:, :LANES], bias2[:, :LANES], offset).astype(BF16)
        c = conv_silu(c_raw, taps2[:, LANES:], bias2[:, LANES:], offset).astype(BF16)
        raw_step = step[q, pl.ds(pl.multiple_of(at + TILE, TILE), PAGE), :]
        v = raw_step + dt_bias
        dt = jnp.maximum(v, 0.0) + jnp.log1p(jnp.exp(-jnp.abs(v)))
        log_rate = rate * dt
        cum = dot(below, log_rate, precision=HIGHEST)
        last = cum[PAGE - 1 : PAGE, :]
        kept = (row >= opened - first).astype(F32)
        weight = jnp.exp(last - cum) * dt * kept
        cum_t = cum.T
        x_ref[i] = x.astype(BF16)
        b_ref[i] = b
        c_ref[i] = c
        cum_ref[i] = cum
        dt_ref[i] = dt
        whole = jnp.broadcast_to(jnp.exp(cum_t[0:8, PAGE - 1 : PAGE]), (8, LANES)) * alive
        for pair in range(pairs):
            scaled = (x[:, pair * LANES : (pair + 1) * LANES] * pair_columns(weight, pair)).astype(BF16)
            added = dot(scaled, b, TN)
            for k in (0, 1):
                h = 2 * pair + k
                here = slice(h * 64, (h + 1) * 64)
                state[here, :] = state[here, :] * whole[h : h + 1, :] + added[k * 64 : (k + 1) * 64, :]
        for k in range(len(starts)):
            start = starts[k]

            @pl.when((start >= first) & (start == opened))
            def _():
                before = jnp.sum(jnp.where(col == start - first - 1, cum_t, 0.0), axis=1, keepdims=True)
                opening = jnp.exp(cum_t[0:8, PAGE - 1 : PAGE] - before[0:8])
                opening = jnp.broadcast_to(opening, (8, LANES))
                for h in range(heads):
                    here = slice(h * 64, (h + 1) * 64)
                    state[here, :] = state[here, :] + opening[h : h + 1, :] * init[groups[k], here, :]

        factor[...] = factor[...] * whole
        end_ref[i] = state[...]
        factor_ref[i] = factor[...]

        @pl.when(i % per_run == per_run - 1)
        def _():
            summary_ref[i // per_run, : heads * 64, :] = state[...].astype(BF16)
            tail = jnp.concatenate([factor[...], jnp.zeros_like(factor[...])], axis=0)
            summary_ref[i // per_run, heads * 64 :, :] = tail.astype(BF16)

        return carry

    lax.fori_loop(0, chunks, one, 0)


def within_kernel(heads, tokens, sizes, ints, x_ref, b_ref, c_ref, cum_ref, dt_ref, params, init, y_ref):
    info, _, lengths, groups = views(ints, sizes)[:4]
    starts = starts_of(lengths)
    skip = head_lanes(params[8:16, 2 * N : 2 * N + LANES], heads, info)[2:3]
    skip = jnp.broadcast_to(skip, (PAGE, LANES))
    chunks = x_ref.shape[0]
    pairs = heads // 2
    row = lax.broadcasted_iota(jnp.int32, (PAGE, PAGE), 0)
    col = lax.broadcasted_iota(jnp.int32, (PAGE, PAGE), 1)
    lane = lax.broadcasted_iota(jnp.int32, (PAGE, LANES), 1)

    def one(i, carry):
        first = chunk_start(i, info, tokens)
        start_of = first_positions(first, starts, (PAGE, PAGE))
        bias = jnp.where((row >= col) & (col >= start_of - first), 0.0, -1e30)
        b, c = b_ref[i], c_ref[i]
        cum, dt = cum_ref[i], dt_ref[i]
        cum_t = cum.T
        scores = dot(c, b, NT)
        for pair in range(pairs):
            here = slice(pair * LANES, (pair + 1) * LANES)
            x = x_ref[i, :, here].astype(F32)
            scaled = x * pair_columns(dt, pair)
            mixing = []
            for h in (2 * pair, 2 * pair + 1):
                gap = cum[:, h : h + 1] + bias - cum_t[h : h + 1, :]
                mixing.append((scores * jnp.exp(gap)).astype(BF16))
            both = jnp.concatenate(
                [jnp.where(lane < 64, scaled, 0.0), jnp.where(lane < 64, 0.0, scaled)], axis=0
            ).astype(BF16)
            y = dot(jnp.concatenate(mixing, axis=1), both)
            y_ref[i, :, here] = y + pair_columns(skip, pair) * x
        for k in range(len(starts)):
            start = starts[k]

            @pl.when((start >= first) & (start < first + PAGE))
            def _():
                before = jnp.sum(jnp.where(row == start - first - 1, cum, 0.0), axis=0, keepdims=True)
                opening = jnp.exp(jnp.minimum(cum - before, 0.0))
                opening = jnp.where(start_of == start, opening, 0.0)
                for pair in range(pairs):
                    here = slice(pair * LANES, (pair + 1) * LANES)
                    read = dot(c, init[groups[k], here, :].astype(BF16), NT)
                    y_ref[i, :, here] = y_ref[i, :, here] + pair_columns(opening, pair) * read

        return carry

    lax.fori_loop(0, chunks, one, 0)


def onto(run, h, before):
    here = slice(h * 64, (h + 1) * 64)
    decay = run[run.shape[0] - 16 + h : run.shape[0] - 16 + h + 1, :].astype(F32)
    return decay * before + run[here, :].astype(F32)


def compose_kernel(heads, sizes, ints, mine, theirs, block_ref):
    info = views(ints, sizes)[0]
    low = info[4] == 0
    runs = []
    for a in range(2):
        m, q = mine[a].astype(F32), theirs[a].astype(F32)
        runs += [jnp.where(low, m, q), jnp.where(low, q, m)]
    total = runs[0]
    for run in runs[1:]:
        parts = []
        for h in range(heads):
            parts.append(onto(run, h, total[h * 64 : (h + 1) * 64, :]))
        tail = total[heads * 64 :, :] * run[heads * 64 :, :]
        total = jnp.concatenate(parts + [tail], axis=0)
    block_ref[...] = total.astype(BF16)


def finish_kernel(heads, tokens, sizes, ints, mine, theirs, entering, c_ref, cum_ref, end_ref,
                  factor_ref, y_ref, gate, params, mixed_ref, square_ref, page0, page1, page2, page3,
                  starting, state):
    info, _, lengths = views(ints, sizes)[:3]
    starts = starts_of(lengths)
    width = heads * 64
    gain = params[5:6, pl.ds(pl.multiple_of(info[0] * width, LANES), width)]
    pages = (page0, page1, page2, page3)
    chunks = c_ref.shape[0]
    per = tokens // PAGE
    per_run = chunks // 2
    pairs = heads // 2
    me, y = info[0], info[4]
    for h in range(heads):
        here = slice(h * 64, (h + 1) * 64)
        outside = entering[here, :].astype(F32)
        first = jnp.where(y == 0, outside, onto(theirs[0], h, outside))
        starting[0, here, :] = first
        second = onto(mine[0], h, first)
        third = jnp.where(y == 0, onto(theirs[0], h, second), onto(theirs[1], h, second))
        starting[1, here, :] = third
    ones = jnp.ones((8, LANES), F32)

    def one(i, carry):
        run = i // per_run

        @pl.when(i % per_run == 0)
        def _():
            state[...] = starting[run]

        q = i // per
        first = chunk_start(i, info, tokens)
        alive = (first_positions(first, starts, (PAGE, LANES)) < first).astype(F32)
        decay = jnp.exp(cum_ref[i]) * alive
        read = dot(c_ref[i], state[...].astype(BF16), NT)
        rows = pl.ds(pl.multiple_of(TILE + (i % per_run) * PAGE, TILE), PAGE)
        squares = jnp.zeros((PAGE, LANES), F32)
        for pair in range(pairs):
            here = slice(pair * LANES, (pair + 1) * LANES)
            value = y_ref[i, :, here] + pair_columns(decay, pair) * read[:, here]
            value = value * gate[run, rows, here].astype(F32)
            mixed_ref[i, :, here] = (value * gain[:, here]).astype(BF16)
            squares = squares + value * value
        square_ref[i] = dot(ones, squares, NT, HIGHEST)
        for h in range(heads):
            here = slice(h * 64, (h + 1) * 64)
            after = end_ref[i, here, :] + factor_ref[i, h : h + 1, :] * starting[run, here, :]
            state[here, :] = after
        for rel in range(4):

            @pl.when(q ^ me == rel)
            def _():
                pages[rel][i % per] = state[...].astype(BF16)

        return carry

    lax.fori_loop(0, chunks, one, 0)


def columns_kernel(sizes, count, rows, *refs):
    info = views(refs[0], sizes)[0]
    parts = refs[1 : 1 + count]
    out = refs[1 + count]
    for index in range(count):
        for place in range(4):
            seq = stored_block(index // 2, index % 2, 2 * place, info) // 2
            at = pl.multiple_of(seq * rows, TILE)
            out[pl.ds(at, rows), :] = parts[index][place * rows : (place + 1) * rows, :]


def mix_kernel(sizes, keep, ints, mixed, squares, columns, out):
    info = views(ints, sizes)[0]
    me, c = info[0], info[1]
    half = c if keep else 1 - c
    for rel in range(4):
        i = (me ^ rel) * 2 + half
        out[rel, :PAGE, :] = dot(mixed[i], columns[...], NT).astype(BF16)
        both = jnp.concatenate([squares[i], squares[i]], axis=0)
        out[rel, PAGE:, :LANES] = both.astype(BF16)
        out[rel, PAGE:, LANES:] = jnp.zeros((TILE, out.shape[2] - LANES), BF16)


def add_cores_kernel(kept, got, send_b, send_a, keep_b, keep_a):
    mid = send_b.shape[2]
    for k in (0, 1):
        total = kept[2 * k + 1, :, :mid].astype(F32) + got[2 * k + 1, :, :mid].astype(F32)
        send_b[k] = total.astype(BF16)
        keep_b[k] = kept[2 * k, :, :mid].astype(F32) + got[2 * k, :, :mid].astype(F32)
        total = kept[k + 2, :PAGE, mid:].astype(F32) + got[k + 2, :PAGE, mid:].astype(F32)
        send_a[k] = total.astype(BF16)
        keep_a[k] = kept[k, :PAGE, mid:].astype(F32) + got[k, :PAGE, mid:].astype(F32)


def add_second_kernel(keep_b, got_b, keep_a, got_a, send_a, send_b, left, right):
    send_a[...] = (keep_b[1] + got_b[1].astype(F32)).astype(BF16)
    left[...] = keep_b[0] + got_b[0].astype(F32)
    send_b[...] = (keep_a[1] + got_a[1].astype(F32)).astype(BF16)
    right[...] = keep_a[0] + got_a[0].astype(F32)


def add_last_kernel(channels, left, got_left, right, got_right, out):
    mid = left.shape[1]
    squares = left[PAGE : PAGE + 1, :LANES] + got_left[PAGE:, :LANES].astype(F32)[0:1]
    row = lax.broadcasted_iota(jnp.int32, (PAGE, PAGE), 0)
    col = lax.broadcasted_iota(jnp.int32, (PAGE, PAGE), 1)
    squares = jnp.sum(jnp.where(row == col, squares, 0.0), axis=1, keepdims=True)
    scale = lax.rsqrt(squares / channels + EPSILON)
    out[:, :mid] = ((left[:PAGE] + got_left[:PAGE, :].astype(F32)) * scale).astype(BF16)
    out[:, mid:] = ((right[...] + got_right[...].astype(F32)) * scale).astype(BF16)


def page_kernel(sizes, ints, own, from_b, from_a, from_d, out):
    info, _, _, _, table = views(ints, sizes)
    me, seq, per = info[0], info[6], own.shape[0]
    for k in range(per):
        slot = table[k] - seq * per
        for rel, source in enumerate((own, from_b, from_a, from_d)):
            out[slot, me ^ rel] = source[k].astype(F32)


def round_t(x, count):
    return lax.ppermute(x, "t", [(i, (i + 1) % count) for i in range(count)])


def weight_parts(part, count):
    parts = []
    for s in range(count):
        part = round_t(part, count) if s > 0 else part
        parts += [part, swap(part, "y")]
    return parts


def in_order(parts, index):
    stacked = jnp.stack(parts)
    blocks = stacked.reshape((-1, stacked.shape[1] * len(parts) // index.shape[0], stacked.shape[2]))
    return jnp.zeros_like(blocks).at[index].set(blocks).reshape(-1, stacked.shape[2])


def on_device(
    hidden_in,
    gate_proj,
    inner_proj,
    small_proj,
    row_layout,
    conv_inner,
    conv_shared,
    bias_inner,
    bias_shared,
    dt_bias,
    decay_log,
    skip_gain,
    norm_gain,
    out_proj,
    prompt_lengths,
    group_map,
    init_states,
    page_table,
):
    tokens, model = hidden_in.shape
    rows = gate_proj.shape[0]
    half_heads = dt_bias.shape[0]
    heads = half_heads // 4
    inner = conv_inner.shape[1]
    head_dim = inner // half_heads
    width = heads * head_dim
    t_count = lax.axis_size("t")
    t, a, y, b, c = (lax.axis_index(name) for name in ("t", "a", "y", "b", "tp"))
    me = a * 2 + b
    seq = ((t * 2 + a) * 2 + y) * 2 + b
    info = jnp.stack([me, c, 0 * c, t, y, 0 * c + t_count, seq, 0 * c]).astype(jnp.int32)
    pieces = [info, row_layout, prompt_lengths, group_map, page_table]
    sizes = tuple(piece.shape[0] for piece in pieces)
    ints = jnp.concatenate(pieces)
    per_head = jnp.pad(jnp.stack([dt_bias, decay_log, skip_gain]), ((0, 5), (0, LANES - half_heads)))
    top = jnp.concatenate([conv_inner, bias_inner[None], norm_gain[None]])
    low = jnp.concatenate([conv_shared, bias_shared[None]])
    low = jnp.concatenate([jnp.pad(low, ((0, 3), (0, 0))), per_head], axis=1)
    params = jnp.concatenate(
        [jnp.pad(top, ((0, 2), (0, 0))), jnp.pad(low, ((0, 0), (0, inner - low.shape[1])))]
    )
    count = 2 * t_count

    wide = width + N + LANES
    aligned = rows % TILE == 0
    inner_send = call(
        functools.partial(pack_kernel, heads),
        "pack_rows",
        shape((8, rows, wide + width), BF16),
        [inner_proj, small_proj, gate_proj],
    )
    inner_got = lax.all_to_all(inner_send, GROUP, 0, 0, tiled=True)

    size = lax.axis_size(SEQ)
    half = tokens // 2
    mine = lax.dynamic_slice_in_dim(hidden_in, c * half, half, 0)
    mine_b, mine_a = swap(mine, "b"), swap(mine, "a")
    tail = hidden_in[tokens - TILE :]
    halo0 = lax.ppermute(tail, SEQ, [(i, i + 1) for i in range(1, size - 1, 2)])
    halo1 = lax.ppermute(tail, SEQ, [(i, i + 2) for i in range(1, size - 2, 2)])

    if aligned:
        part, low, high, gate_part = call(
            repack_kernel,
            "repack_inner",
            (
                shape((8 * rows + TILE, width + N), BF16),
                shape((4 * rows, width + N), BF16),
                shape((4 * rows + TILE, width + N), BF16),
                shape((8 * rows, width), BF16),
            ),
            [inner_got],
        )
        marks, inner_parts = [(0, 0, 0), (0, 1, 0)], [part, swap(part, "y")]
        for s in range(1, t_count):
            low, high = round_t(low, t_count), round_t(high, t_count)
            marks += [(s, 0, 0), (s, 0, 4), (s, 1, 0), (s, 1, 4)]
            inner_parts += [low, high, swap(low, "y"), swap(high, "y")]
        ready = [part]
    else:
        marks = None
        index = [stored_block(s, dy, p, info) for s in range(t_count) for dy in (0, 1) for p in range(8)]
        index = row_layout[jnp.stack(index)]
        inner_got = inner_got.reshape(8 * rows, wide + width)
        inner_parts = [in_order(weight_parts(inner_got[:, :wide], t_count), index)]
        gate_part = inner_got[:, wide:]
        ready = high = None

    over_b, over_a = call(
        functools.partial(forward_kernel, sizes),
        "forward_rows",
        (shape((half // 2, model), BF16), shape((half // 2 + TILE, model), BF16)),
        [ints, mine_b, mine_a, halo0, halo1],
        after=ready or (),
    )
    mine_d0, mine_d1 = swap(over_b, "b"), swap(over_a, "a")
    rows_in = [mine_b, mine_a, mine_d0, mine_d1]
    hidden = call(
        functools.partial(assemble_kernel, sizes),
        "assemble_rows",
        shape((2, TILE + 2 * tokens, model), BF16),
        [ints, hidden_in, *rows_in, *[swap(x, "tp") for x in rows_in], halo0, halo1],
        us=2,
    )
    if aligned:
        gate_part = call(copy_kernel, "gate_part", shape(gate_part.shape, BF16), [gate_part], after=[high])
    gate_parts = weight_parts(gate_part, t_count)
    out_send = call(
        pack_out_kernel,
        "pack_out",
        shape((4, out_proj.shape[1], width), BF16),
        [out_proj.T],
        after=[high] if aligned else (),
    )
    out_got = lax.all_to_all(out_send, ("a", "b"), 0, 0, tiled=True)
    out_rows = out_proj.shape[1]
    out_got = out_got.reshape(4 * out_rows, width)
    if out_rows % TILE == 0:
        out_got = call(
            copy_kernel, "out_part", shape(out_got.shape, BF16), [out_got], after=[gate_parts[-2]]
        )
    out_parts = weight_parts(out_got, t_count)
    if not aligned:
        gate_parts = [in_order(gate_parts, index)]
    if out_rows % TILE == 0:
        columns = call(
            functools.partial(columns_kernel, sizes, count, out_rows),
            "columns",
            shape((model, width), BF16),
            [ints, *out_parts],
        )
    else:
        index = [
            stored_block(s, dy, 2 * p, info) // 2
            for s in range(t_count)
            for dy in (0, 1)
            for p in range(4)
        ]
        columns = in_order(out_parts, jnp.stack(index))

    long = TILE + 2 * tokens
    raw, shared, step = call(
        functools.partial(inner_kernel, sizes, marks, rows),
        "inner_projection",
        (
            shape((2, long, width), BF16),
            shape((2, long, LANES), BF16),
            shape((2, long, LANES), F32),
        ),
        [ints, hidden, *inner_parts],
        [pltpu.VMEM((model, wide), BF16)] if marks else [], us=4.3
    )
    shared_other = swap(shared, "tp")
    init = lax.dynamic_slice_in_dim(init_states, me * heads, heads, 1)
    init = init.reshape(init.shape[0], width, N)
    chunks = 4 * tokens // PAGE
    x, b_in, c_in, cum, dt, ends, factors, summary = call(
        functools.partial(state_kernel, heads, tokens, sizes),
        "states",
        (
            shape((chunks, PAGE, width), BF16),
            shape((chunks, PAGE, N), BF16),
            shape((chunks, PAGE, N), BF16),
            shape((chunks, PAGE, LANES), F32),
            shape((chunks, PAGE, LANES), F32),
            shape((chunks, width, N), F32),
            shape((chunks, 8, N), F32),
            shape((2, width + 16, N), BF16),
        ),
        [ints, raw, shared, shared_other, step, params, init],
        [pltpu.VMEM((width, N), F32), pltpu.VMEM((8, N), F32)], us=9.3
    )
    theirs = swap(summary, "y")
    block = call(
        functools.partial(compose_kernel, heads, sizes),
        "compose",
        shape((width + 16, N), BF16),
        [ints, summary, theirs],
    )
    onward = [(i, i + 1) for i in range(t_count - 1)]
    gate_marks = [(s, dy, 0) for s in range(t_count) for dy in (0, 1)] if aligned else None
    gate = call(
        functools.partial(gate_kernel, sizes, gate_marks, rows),
        "gate_projection",
        shape((2, long, width), BF16),
        [ints, hidden, *gate_parts],
        [pltpu.VMEM((model, width), BF16)] if aligned else [],
        after=[block], us=3
    )
    block = lax.ppermute(block, "t", onward)
    entering = block
    if t_count > 2:
        total = block[:width].astype(F32).reshape(heads, head_dim, N)
        decay = block[width : width + heads, None, :].astype(F32)
        for _ in range(t_count - 2):
            block = lax.ppermute(block, "t", onward)
            total = total + decay * block[:width].astype(F32).reshape(heads, head_dim, N)
            decay = decay * block[width : width + heads, None, :].astype(F32)
        entering = total.reshape(width, N)
    y_within = call(
        functools.partial(within_kernel, heads, tokens, sizes),
        "within_chunks",
        shape((chunks, PAGE, width), F32),
        [ints, x, b_in, c_in, cum, dt, params, init], us=5.4
    )
    mixed, squares, *pages = call(
        functools.partial(finish_kernel, heads, tokens, sizes),
        "finish",
        (
            shape((chunks, PAGE, width), BF16),
            shape((chunks, 8, PAGE), F32),
            *[shape((tokens // PAGE, width, N), BF16)] * 4,
        ),
        [ints, summary, theirs, entering, c_in, cum, ends, factors, y_within, gate, params],
        [pltpu.VMEM((2, width, N), F32), pltpu.VMEM((width, N), F32)], us=4.8
    )

    across = [(i, i ^ 3) for i in range(4)]
    got = [pages[0], swap(pages[1], "b"), swap(pages[2], "a"), lax.ppermute(pages[3], ("a", "b"), across)]
    per = tokens // PAGE
    state_pages = call(
        functools.partial(page_kernel, sizes), "pages", shape((per, 4, width, N), F32), [ints, *got], us=1.8
    ).reshape(per, half_heads, head_dim, N)

    dims = shape((4, PAGE + TILE, model), BF16)
    sent = call(functools.partial(mix_kernel, sizes, False), "mix_send", dims, [ints, mixed, squares, columns], us=2.1)
    got = swap(sent, "tp")
    kept = call(functools.partial(mix_kernel, sizes, True), "mix_keep", dims, [ints, mixed, squares, columns], us=2.1)
    mid = model // 2
    send_b, send_a, keep_b, keep_a = call(
        add_cores_kernel,
        "add_cores",
        (
            shape((2, PAGE + TILE, mid), BF16),
            shape((2, PAGE, mid), BF16),
            shape((2, PAGE + TILE, mid), F32),
            shape((2, PAGE, mid), F32),
        ),
        [kept, got],
    )
    got_b, got_a = swap(send_b, "b"), swap(send_a, "a")
    send_a, send_b, left, right = call(
        add_second_kernel,
        "add_second",
        (
            shape((PAGE + TILE, mid), BF16),
            shape((PAGE, mid), BF16),
            shape((PAGE + TILE, mid), F32),
            shape((PAGE, mid), F32),
        ),
        [keep_b, got_b, keep_a, got_a],
    )
    got_left, got_right = swap(send_a, "a"), swap(send_b, "b")
    mixed_out = call(
        functools.partial(add_last_kernel, float(2 * inner)),
        "add_last",
        shape((PAGE, model), BF16),
        [left, got_left, right, got_right],
    )
    return (mixed_out, state_pages)


def solution(mesh):
    count = mesh.shape["seq"]
    fine = Mesh(mesh.devices.reshape(count // 8, 2, 2, 2, 2), SEQ + ("tp",))
    placed = (
        P(SEQ, None),
        P(SEQ + ("tp",), None),
        P(SEQ + ("tp",), None),
        P(SEQ + ("tp",), None),
        P(),
        P(None, "tp"),
        P(),
        P("tp"),
        P(),
        P("tp"),
        P("tp"),
        P("tp"),
        P("tp"),
        P("tp", SEQ),
        P(),
        P(),
        P(None, "tp", None, None),
        P(SEQ),
    )
    return jax.shard_map(
        on_device,
        mesh=fine,
        in_specs=placed,
        out_specs=(P(SEQ + ("tp",), None), P(SEQ, "tp", None, None)),
        check_vma=False,
    )
```

```python
import functools

import jax
import jax.numpy as jnp
from jax import lax
from jax.experimental import pallas as pl
from jax.experimental.pallas import tpu as pltpu
from jax.sharding import Mesh
from jax.sharding import PartitionSpec as P

N = 128
CONV = 4
PAGE = 128
TILE = 16
LANES = 128
EPSILON = 1e-05
F32 = jnp.float32
BF16 = jnp.bfloat16
HIGHEST = lax.Precision.HIGHEST
GROUP = ("a", "b", "tp")
SEQ = ("t", "a", "y", "b")
VMEM = pl.BlockSpec(memory_space=pltpu.VMEM)
SMEM = pl.BlockSpec(memory_space=pltpu.SMEM)
ANY = pl.BlockSpec(memory_space=pl.ANY)


def call(body, name, out_shape, ins, scratch=(), after=(), us=1.0, limit=16,
         fetch=False):
    specs = [SMEM if x.dtype == jnp.int32 else (ANY if fetch else VMEM) for x in ins]
    specs += [ANY] * len(after)
    first, last = len(ins), len(ins) + len(after)

    def kernel(*refs):
        body(*refs[:first], *refs[last:])

    return pl.pallas_call(
        kernel,
        name=name,
        out_shape=out_shape,
        in_specs=specs,
        out_specs=jax.tree.map(lambda _: VMEM, out_shape),
        scratch_shapes=list(scratch),
        cost_estimate=pl.CostEstimate(
            flops=int(us * 1e9), bytes_accessed=int(us * 3e6), transcendentals=0
        ),
        compiler_params=pltpu.CompilerParams(vmem_limit_bytes=limit << 20),
    )(*ins, *after)


def shape(dims, dtype):
    return jax.ShapeDtypeStruct(dims, dtype)


def dot(x, y, dims=((1,), (0,)), precision=None):
    return lax.dot_general(x, y, (dims, ((), ())), precision=precision, preferred_element_type=F32)


NT = ((1,), (1,))
TN = ((0,), (0,))


def swap(x, axis):
    return lax.ppermute(x, axis, [(0, 1), (1, 0)])


class Ints:
    def __init__(self, ref, at, size):
        self.ref, self.at, self.size = ref, at, size

    def __getitem__(self, k):
        return self.ref[self.at + k]


def views(ref, sizes):
    out, at = [], 0
    for size in sizes:
        out.append(Ints(ref, at, size))
        at += size
    return out


def stored_block(s, dy, place, info):
    t, y, count = info[3], info[4], info[5]
    a, b, c = place // 4, (place // 2) % 2, place % 2
    source = lax.rem(t - s + count, count)
    seq = ((source * 2 + a) * 2 + (y ^ dy)) * 2 + b
    return seq * 2 + c


def pack_kernel(heads, inner_hbm, small_hbm, gate_hbm, out, inner, small, gate, arrived):
    copies = [
        pltpu.make_async_copy(source, target, arrived.at[k])
        for k, (source, target) in enumerate(((inner_hbm, inner), (small_hbm, small), (gate_hbm, gate)))
    ]
    for copy in copies:
        copy.start()
    width = heads * 64
    rows = inner.shape[0]
    places = [(place, place % 2, place // 2) for place in range(8)]
    copies[0].wait()
    for place, c, group in places:
        at = (c * 4 + group) * width
        out[place, :, :width] = inner[:, at : at + width].astype(BF16)
    copies[1].wait()
    lane = lax.broadcasted_iota(jnp.int32, (rows, LANES), 1)
    steps = small[:, 2 * N :]
    steps = jnp.concatenate([steps, jnp.zeros((rows, LANES - steps.shape[1]), F32)], axis=1)
    for place, c, group in places:
        out[place, :, width : width + N] = small[:, c * N : (c + 1) * N].astype(BF16)
        first = (c * 4 + group) * heads
        moved = pltpu.roll(steps, LANES - first, 1) if first else steps
        out[place, :, width + N : width + N + LANES] = jnp.where(lane < heads, moved, 0.0).astype(BF16)
    copies[2].wait()
    for place, c, group in places:
        at = (c * 4 + group) * width
        out[place, :, width + N + LANES :] = gate[:, at : at + width].astype(BF16)


def rows_kernel(sizes, ints, hidden, mine, tail, arrived):
    c = views(ints, sizes)[0][1]
    half = mine.shape[0]
    at = pl.multiple_of(c * half, TILE)
    copies = (
        pltpu.make_async_copy(hidden.at[pl.ds(at, half), :], mine, arrived.at[0]),
        pltpu.make_async_copy(hidden.at[pl.ds(hidden.shape[0] - TILE, TILE), :], tail, arrived.at[1]),
    )
    for copy in copies:
        copy.start()
    for copy in copies:
        copy.wait()


def repack_kernel(got, whole, low, high, gate):
    rows, width = got.shape[1], whole.shape[1]
    cut = low.shape[0] // rows
    for place in range(8):
        gate[place * rows : (place + 1) * rows, :] = got[place, :, width + LANES :]
    lane = lax.broadcasted_iota(jnp.int32, (TILE, LANES), 1) // TILE
    for place in range(8):
        block = got[place, :, :width]
        whole[place * rows : (place + 1) * rows, :] = block
        half, at = (low, place) if place < cut else (high, place - cut)
        half[at * rows : (at + 1) * rows, :] = block
    for piece in range(rows // TILE):
        packed = jnp.zeros((TILE, LANES), F32)
        for place in range(8):
            steps = got[place, piece * TILE : (piece + 1) * TILE, width : width + LANES].astype(F32)
            steps = pltpu.roll(steps, place * TILE, 1) if place else steps
            packed = jnp.where(lane == place, steps, packed)
        here = slice(piece * LANES, (piece + 1) * LANES)
        whole[8 * rows :, here] = packed.astype(BF16)
        high[(8 - cut) * rows :, here] = packed.astype(BF16)
    rest = rows // TILE * LANES
    if rest < width:
        blank = jnp.zeros((TILE, width - rest), BF16)
        whole[8 * rows :, rest:] = blank
        high[(8 - cut) * rows :, rest:] = blank


def copy_kernel(source, out):
    out[...] = source[...]


def pack_out_kernel(sizes, ints, source, *outs):
    me = views(ints, sizes)[0][0]
    width = outs[0].shape[1]
    for rel, out in enumerate(outs):
        at = pl.multiple_of((me ^ rel) * width, LANES)
        out[...] = source[:, pl.ds(at, width)].astype(BF16)


def join_kernel(*refs):
    out, at = refs[-1], 0
    for source in refs[:-1]:
        out[at : at + source.shape[0], :] = source[...]
        at += source.shape[0]


def forward_kernel(sizes, ints, mine_b, mine_a, halo0, halo1, over_b, over_a):
    info = views(ints, sizes)[0]
    cut = over_b.shape[0]
    over_b[...] = mine_a[:cut, :]
    over_a[:cut, :] = mine_b[cut:, :]

    @pl.when(info[0] % 2 == 0)
    def _():
        over_a[cut:, :] = halo0[...]

    @pl.when(info[0] % 2 == 1)
    def _():
        over_a[cut:, :] = halo1[...]


def assemble_kernel(sizes, ints, own, mine_b, mine_a, mine_d0, mine_d1, other_b, other_a, other_d0,
                    other_d1, halo0, halo1, out):
    info = views(ints, sizes)[0]
    me, c = info[0], info[1]
    half = own.shape[0] // 2

    def put(q, h, row, source):
        at = TILE + ((q % 2) * 2 + h) * half + row
        out[q // 2, pl.ds(pl.multiple_of(at, TILE), source.shape[0]), :] = source

    put(me, 0, 0, own[:half, :])
    put(me, 1, 0, own[half:, :])
    for h, parts in ((c, (mine_b, mine_a, mine_d0, mine_d1)), (1 - c, (other_b, other_a, other_d0, other_d1))):
        cut = parts[2].shape[0]
        put(me ^ 1, h, 0, parts[0][...])
        put(me ^ 2, h, 0, parts[1][...])
        put(me ^ 3, h, 0, parts[2][...])
        put(me ^ 3, h, cut, parts[3][:cut, :])
    a = me // 2
    out[1 - a, :TILE, :] = mine_d1[cut:, :]

    @pl.when(me % 2 == 0)
    def _():
        out[a, :TILE, :] = halo0[...]

    @pl.when(me % 2 == 1)
    def _():
        out[a, :TILE, :] = halo1[...]


def place_parts(weights, marks, rows, parts, info, layout):
    width = parts[0].shape[1]
    lane = lax.broadcasted_iota(jnp.int32, (TILE, LANES), 1) // TILE
    for (s, dy, first), part in zip(marks, parts):
        count = part.shape[0] // rows
        for k in range(count):
            block = layout[stored_block(s, dy, first + k, info)]
            at = pl.multiple_of(block * rows, TILE)
            weights[pl.ds(at, rows), :width] = part[k * rows : (k + 1) * rows, :]
        base = count * rows
        if part.shape[0] == base:
            continue
        for place in range(8):
            block = layout[stored_block(s, dy, place, info)]
            for piece in range(rows // TILE):
                packed = part[base : base + TILE, piece * LANES : (piece + 1) * LANES]
                kept = jnp.where(lane == place, packed, jnp.zeros_like(packed))
                at = pl.multiple_of(block * rows + piece * TILE, TILE)
                weights[pl.ds(at, TILE), width:] = kept


def weights_kernel(sizes, marks, rows, *refs):
    info, layout = views(refs[0], sizes)[:2]
    place_parts(refs[1 + len(marks)], marks, rows, refs[1 : 1 + len(marks)], info, layout)


def inner_kernel(hidden, weights, raw_ref, shared_ref, step_ref):
    bc = raw_ref.shape[2]
    for run in range(2):
        result = dot(hidden[run], weights[:, bc:])
        shared_ref[run] = result[:, :LANES].astype(BF16)
        step = result[:, LANES:]
        for shift in (64, 32, 16):
            step = step + pltpu.roll(step, shift, 1)
        step_ref[run] = step
        raw_ref[run] = dot(hidden[run], weights[:, :bc]).astype(BF16)


def gate_kernel(hidden, weights, gate_ref):
    for run in range(2):
        gate_ref[run] = jax.nn.silu(dot(hidden[run], weights[...])).astype(BF16)


def starts_of(lengths):
    starts, total = [], jnp.int32(0)
    for k in range(lengths.size):
        starts.append(total)
        total = total + lengths[k]
    return starts


def head_lanes(row, heads, info):
    return pltpu.roll(row, lax.rem(LANES - info[0] * heads, LANES), 1)


def chunk_start(i, info, tokens):
    t, y = info[3], info[4]
    per = tokens // PAGE
    q = i // per
    seq = ((t * 2 + q // 2) * 2 + y) * 2 + q % 2
    return seq * tokens + (i % per) * PAGE


def last_start(position, starts):
    best = jnp.int32(0)
    for k in range(len(starts)):
        best = jnp.maximum(best, jnp.where(starts[k] <= position, starts[k], 0))
    return best


def first_positions(first, starts, dims):
    position = first + lax.broadcasted_iota(jnp.int32, dims, 0)
    best = jnp.zeros(dims, jnp.int32)
    for k in range(len(starts)):
        best = jnp.maximum(best, jnp.where(starts[k] <= position, starts[k], 0))
    return best


def conv_silu(window, taps, bias, offset):
    total = bias + taps[0:1, :] * window[TILE : TILE + PAGE]
    for lag in range(1, CONV):
        within = (offset >= lag).astype(F32)
        total = total + taps[lag : lag + 1, :] * window[TILE - lag : TILE - lag + PAGE] * within
    return total / (1.0 + jnp.exp(-total))


def pair_columns(values, pair):
    lane = lax.broadcasted_iota(jnp.int32, (PAGE, LANES), 1)
    left = values[:, 2 * pair : 2 * pair + 1]
    right = values[:, 2 * pair + 1 : 2 * pair + 2]
    return jnp.where(lane < 64, left, right)


def state_kernel(heads, tokens, sizes, ints, raw, own, other, step, params, init, x_ref, b_ref, c_ref,
                 cum_ref, dt_ref, end_ref, factor_ref, summary_ref):
    info, _, lengths, groups = views(ints, sizes)[:4]
    starts = starts_of(lengths)
    width = heads * 64
    here = pl.ds(pl.multiple_of(info[0] * width, LANES), width)
    taps, bias = params[0:4, here], params[4:5, here]
    taps2, bias2 = params[8:12, : 2 * N], params[12:13, : 2 * N]
    per_head = head_lanes(params[8:16, 2 * N : 2 * N + LANES], heads, info)
    dt_bias, rate = per_head[0:1], -jnp.exp(per_head[1:2])
    chunks = x_ref.shape[0]
    per_run = chunks // 2
    pairs = heads // 2
    row = lax.broadcasted_iota(jnp.int32, (PAGE, PAGE), 0)
    col = lax.broadcasted_iota(jnp.int32, (PAGE, PAGE), 1)
    below = (row >= col).astype(F32)

    def one(i, carry):
        first = chunk_start(i, info, tokens)
        opened = last_start(first + PAGE - 1, starts)
        alive = (opened < first).astype(F32)
        start_of = first_positions(first, starts, (PAGE, 1))
        offset = first + lax.broadcasted_iota(jnp.int32, (PAGE, 1), 0) - start_of
        q = i // per_run
        at = pl.multiple_of((i % per_run) * PAGE, TILE)
        window = pl.ds(at, PAGE + TILE)
        x = conv_silu(raw[q, window, :].astype(F32), taps, bias, offset)
        is_first = info[1] == 0
        mine, theirs = own[q, window, :].astype(F32), other[q, window, :].astype(F32)
        b_raw = jnp.where(is_first, mine, theirs)
        c_raw = jnp.where(is_first, theirs, mine)
        b = conv_silu(b_raw, taps2[:, :LANES], bias2[:, :LANES], offset).astype(BF16)
        c = conv_silu(c_raw, taps2[:, LANES:], bias2[:, LANES:], offset).astype(BF16)
        raw_step = step[q, pl.ds(pl.multiple_of(at + TILE, TILE), PAGE), :]
        v = raw_step + dt_bias
        dt = jnp.maximum(v, 0.0) + jnp.log1p(jnp.exp(-jnp.abs(v)))
        log_rate = rate * dt
        cum = dot(below, log_rate, precision=HIGHEST)
        last = cum[PAGE - 1 : PAGE, :]
        kept = (row >= opened - first).astype(F32)
        weight = jnp.exp(last - cum) * dt * kept
        cum_t = cum.T
        x_ref[i] = x.astype(BF16)
        b_ref[i] = b
        c_ref[i] = c
        cum_ref[i] = cum
        dt_ref[i] = dt
        last_t = cum_t[0:8, PAGE - 1 : PAGE]
        factor_ref[i] = jnp.broadcast_to(jnp.exp(last_t), (8, LANES)) * alive
        for pair in range(pairs):
            here = slice(pair * LANES, (pair + 1) * LANES)
            scaled = (x[:, here] * pair_columns(weight, pair)).astype(BF16)
            end_ref[i, here, :] = dot(scaled, b, TN)

        @pl.when(opened >= first)
        def _():
            for k in range(len(starts)):

                @pl.when(starts[k] == opened)
                def _():
                    at_start = col == opened - first - 1
                    before = jnp.sum(jnp.where(at_start, cum_t, 0.0), axis=1, keepdims=True)
                    opening = jnp.broadcast_to(jnp.exp(last_t - before[0:8]), (8, LANES))
                    for h in range(heads):
                        here = slice(h * 64, (h + 1) * 64)
                        entered = opening[h : h + 1, :] * init[groups[k], here, :]
                        end_ref[i, here, :] = end_ref[i, here, :] + entered

        return carry

    lax.fori_loop(0, chunks, one, 0, unroll=2)
    for run in range(2):
        factor = factor_ref[run * per_run]
        for i in range(run * per_run + 1, (run + 1) * per_run):
            for h in range(heads):
                here = slice(h * 64, (h + 1) * 64)
                end_ref[i, here, :] = end_ref[i, here, :] + factor_ref[i, h : h + 1, :] * end_ref[i - 1, here, :]
            factor = factor * factor_ref[i]
            factor_ref[i] = factor
        summary_ref[run, : heads * 64, :] = end_ref[(run + 1) * per_run - 1].astype(BF16)
        tail = jnp.concatenate([factor, jnp.zeros_like(factor)], axis=0)
        summary_ref[run, heads * 64 :, :] = tail.astype(BF16)


def within_kernel(heads, tokens, sizes, ints, x_ref, b_ref, c_ref, cum_ref, dt_ref, params, init, y_ref):
    info, _, lengths, groups = views(ints, sizes)[:4]
    starts = starts_of(lengths)
    skip = head_lanes(params[8:16, 2 * N : 2 * N + LANES], heads, info)[2:3]
    skip = jnp.broadcast_to(skip, (PAGE, LANES))
    chunks = x_ref.shape[0]
    pairs = heads // 2
    row = lax.broadcasted_iota(jnp.int32, (PAGE, PAGE), 0)
    col = lax.broadcasted_iota(jnp.int32, (PAGE, PAGE), 1)
    lane = lax.broadcasted_iota(jnp.int32, (PAGE, LANES), 1)

    def one(i, carry):
        first = chunk_start(i, info, tokens)
        start_of = first_positions(first, starts, (PAGE, PAGE))
        bias = jnp.where((row >= col) & (col >= start_of - first), 0.0, -1e30)
        b, c = b_ref[i], c_ref[i]
        cum, dt = cum_ref[i], dt_ref[i]
        cum_t = cum.T
        scores = dot(c, b, NT)
        for pair in range(pairs):
            here = slice(pair * LANES, (pair + 1) * LANES)
            x = x_ref[i, :, here].astype(F32)
            scaled = x * pair_columns(dt, pair)
            mixing = []
            for h in (2 * pair, 2 * pair + 1):
                gap = cum[:, h : h + 1] + bias - cum_t[h : h + 1, :]
                mixing.append((scores * jnp.exp(gap)).astype(BF16))
            both = jnp.concatenate(
                [jnp.where(lane < 64, scaled, 0.0), jnp.where(lane < 64, 0.0, scaled)], axis=0
            ).astype(BF16)
            y = dot(jnp.concatenate(mixing, axis=1), both)
            y_ref[i, :, here] = y + pair_columns(skip, pair) * x
        @pl.when(last_start(first + PAGE - 1, starts) >= first)
        def _():
            for k in range(len(starts)):
                start = starts[k]

                @pl.when((start >= first) & (start < first + PAGE))
                def _():
                    at_start = row == start - first - 1
                    before = jnp.sum(jnp.where(at_start, cum, 0.0), axis=0, keepdims=True)
                    opening = jnp.exp(jnp.minimum(cum - before, 0.0))
                    opening = jnp.where(start_of == start, opening, 0.0)
                    for pair in range(pairs):
                        here = slice(pair * LANES, (pair + 1) * LANES)
                        read = dot(c, init[groups[k], here, :].astype(BF16), NT)
                        y_ref[i, :, here] = y_ref[i, :, here] + pair_columns(opening, pair) * read

        return carry

    lax.fori_loop(0, chunks, one, 0, unroll=2)


def onto(run, h, before):
    here = slice(h * 64, (h + 1) * 64)
    decay = run[run.shape[0] - 16 + h : run.shape[0] - 16 + h + 1, :].astype(F32)
    return decay * before + run[here, :].astype(F32)


def compose_kernel(heads, sizes, ints, mine, theirs, block_ref):
    info = views(ints, sizes)[0]
    low = info[4] == 0
    runs = []
    for a in range(2):
        m, q = mine[a].astype(F32), theirs[a].astype(F32)
        runs += [jnp.where(low, m, q), jnp.where(low, q, m)]
    total = runs[0]
    for run in runs[1:]:
        parts = []
        for h in range(heads):
            parts.append(onto(run, h, total[h * 64 : (h + 1) * 64, :]))
        tail = total[heads * 64 :, :] * run[heads * 64 :, :]
        total = jnp.concatenate(parts + [tail], axis=0)
    block_ref[...] = total.astype(BF16)


def enter_kernel(heads, tokens, sizes, ints, mine, theirs, entering, end_ref, factor_ref, states,
                 page0, page1, page2, page3, starting):
    info = views(ints, sizes)[0]
    me, y = info[0], info[4]
    per = tokens // PAGE
    per_run = states.shape[0] // 2
    for h in range(heads):
        here = slice(h * 64, (h + 1) * 64)
        outside = entering[here, :].astype(F32)
        first = jnp.where(y == 0, outside, onto(theirs[0], h, outside))
        starting[0, here, :] = first
        second = onto(mine[0], h, first)
        third = jnp.where(y == 0, onto(theirs[0], h, second), onto(theirs[1], h, second))
        starting[1, here, :] = third
    states[0] = starting[0].astype(BF16)
    states[per_run] = starting[1].astype(BF16)
    for rel, page in enumerate((page0, page1, page2, page3)):
        for k in range(per):
            i = (me ^ rel) * per + k
            run = i // per_run
            for h in range(heads):
                here = slice(h * 64, (h + 1) * 64)
                after = end_ref[i, here, :] + factor_ref[i, h : h + 1, :] * starting[run, here, :]
                page[k, here, :] = after.astype(BF16)

            @pl.when(i % per_run < per_run - 1)
            def _():
                states[i + 1] = page[k]


def finish_kernel(heads, tokens, sizes, ints, states, c_ref, cum_ref, y_ref, gate, params, mixed_ref,
                  square_ref):
    info, _, lengths = views(ints, sizes)[:3]
    starts = starts_of(lengths)
    width = heads * 64
    gain = params[5:6, pl.ds(pl.multiple_of(info[0] * width, LANES), width)]
    chunks = c_ref.shape[0]
    per_run = chunks // 2
    pairs = heads // 2
    ones = jnp.ones((8, LANES), F32)

    def one(i, carry):
        run = i // per_run
        first = chunk_start(i, info, tokens)
        alive = (first_positions(first, starts, (PAGE, LANES)) < first).astype(F32)
        decay = jnp.exp(cum_ref[i]) * alive
        read = dot(c_ref[i], states[i], NT)
        rows = pl.ds(pl.multiple_of(TILE + (i % per_run) * PAGE, TILE), PAGE)
        squares = jnp.zeros((PAGE, LANES), F32)
        for pair in range(pairs):
            here = slice(pair * LANES, (pair + 1) * LANES)
            value = y_ref[i, :, here] + pair_columns(decay, pair) * read[:, here]
            value = value * gate[run, rows, here].astype(F32)
            mixed_ref[i, :, here] = (value * gain[:, here]).astype(BF16)
            squares = squares + value * value
        square_ref[i] = dot(ones, squares, NT, HIGHEST)
        return carry

    lax.fori_loop(0, chunks, one, 0, unroll=2)


def columns_kernel(sizes, count, rows, ints, *refs):
    info = views(ints, sizes)[0]
    parts, out = refs[:count], refs[count]
    for index, part in enumerate(parts):
        for rel in range(4):
            seq = stored_block(index // 2, index % 2, 2 * (info[0] ^ rel), info) // 2
            at = pl.multiple_of(seq * rows, TILE)
            out[pl.ds(at, rows), :] = part[rel * rows : (rel + 1) * rows, :]


def mix_kernel(sizes, keep, ints, mixed, squares, columns, out):
    info = views(ints, sizes)[0]
    me, c = info[0], info[1]
    half = c if keep else 1 - c
    for rel in range(4):
        i = (me ^ rel) * 2 + half
        out[rel, :PAGE, :] = dot(mixed[i], columns[...], NT).astype(BF16)
        both = jnp.concatenate([squares[i], squares[i]], axis=0)
        out[rel, PAGE:, :LANES] = both.astype(BF16)
        out[rel, PAGE:, LANES:] = jnp.zeros((TILE, out.shape[2] - LANES), BF16)


def add_cores_kernel(kept, got, send_b, send_a, keep_b, keep_a):
    mid = send_b.shape[2]
    for k in (0, 1):
        total = kept[2 * k + 1, :, :mid].astype(F32) + got[2 * k + 1, :, :mid].astype(F32)
        send_b[k] = total.astype(BF16)
        keep_b[k] = kept[2 * k, :, :mid].astype(F32) + got[2 * k, :, :mid].astype(F32)
        total = kept[k + 2, :PAGE, mid:].astype(F32) + got[k + 2, :PAGE, mid:].astype(F32)
        send_a[k] = total.astype(BF16)
        keep_a[k] = kept[k, :PAGE, mid:].astype(F32) + got[k, :PAGE, mid:].astype(F32)


def add_second_kernel(keep_b, got_b, keep_a, got_a, send_a, send_b, left, right):
    send_a[...] = (keep_b[1] + got_b[1].astype(F32)).astype(BF16)
    left[...] = keep_b[0] + got_b[0].astype(F32)
    send_b[...] = (keep_a[1] + got_a[1].astype(F32)).astype(BF16)
    right[...] = keep_a[0] + got_a[0].astype(F32)


def add_last_kernel(channels, left, got_left, right, got_right, out):
    mid = left.shape[1]
    squares = left[PAGE : PAGE + 1, :LANES] + got_left[PAGE:, :LANES].astype(F32)[0:1]
    row = lax.broadcasted_iota(jnp.int32, (PAGE, PAGE), 0)
    col = lax.broadcasted_iota(jnp.int32, (PAGE, PAGE), 1)
    squares = jnp.sum(jnp.where(row == col, squares, 0.0), axis=1, keepdims=True)
    scale = lax.rsqrt(squares / channels + EPSILON)
    out[:, :mid] = ((left[:PAGE] + got_left[:PAGE, :].astype(F32)) * scale).astype(BF16)
    out[:, mid:] = ((right[...] + got_right[...].astype(F32)) * scale).astype(BF16)


def page_kernel(sizes, ints, own, from_b, from_a, from_d, out):
    info, _, _, _, table = views(ints, sizes)
    me, seq, per = info[0], info[6], own.shape[0]
    for k in range(per):
        slot = table[k] - seq * per
        for rel, source in enumerate((own, from_b, from_a, from_d)):
            out[slot, me ^ rel] = source[k].astype(F32)


def round_t(x, count):
    return lax.ppermute(x, "t", [(i, (i + 1) % count) for i in range(count)])


def weight_parts(part, count):
    parts = []
    for s in range(count):
        part = round_t(part, count) if s > 0 else part
        parts += [part, swap(part, "y")]
    return parts


def in_order(parts, index):
    stacked = jnp.stack(parts)
    blocks = stacked.reshape((-1, stacked.shape[1] * len(parts) // index.shape[0], stacked.shape[2]))
    return jnp.zeros_like(blocks).at[index].set(blocks).reshape(-1, stacked.shape[2])


def on_device(
    hidden_in,
    gate_proj,
    inner_proj,
    small_proj,
    row_layout,
    conv_inner,
    conv_shared,
    bias_inner,
    bias_shared,
    dt_bias,
    decay_log,
    skip_gain,
    norm_gain,
    out_proj,
    prompt_lengths,
    group_map,
    init_states,
    page_table,
):
    tokens, model = hidden_in.shape
    rows = gate_proj.shape[0]
    half_heads = dt_bias.shape[0]
    heads = half_heads // 4
    inner = conv_inner.shape[1]
    head_dim = inner // half_heads
    width = heads * head_dim
    t_count = lax.axis_size("t")
    t, a, y, b, c = (lax.axis_index(name) for name in ("t", "a", "y", "b", "tp"))
    me = a * 2 + b
    seq = ((t * 2 + a) * 2 + y) * 2 + b
    info = jnp.stack([me, c, 0 * c, t, y, 0 * c + t_count, seq, 0 * c]).astype(jnp.int32)
    pieces = [info, row_layout, prompt_lengths, group_map, page_table]
    sizes = tuple(piece.shape[0] for piece in pieces)
    ints = jnp.concatenate(pieces)
    per_head = jnp.pad(jnp.stack([dt_bias, decay_log, skip_gain]), ((0, 5), (0, LANES - half_heads)))
    top = jnp.concatenate([conv_inner, bias_inner[None], norm_gain[None]])
    low = jnp.concatenate([conv_shared, bias_shared[None]])
    low = jnp.concatenate([jnp.pad(low, ((0, 3), (0, 0))), per_head], axis=1)
    params = jnp.concatenate(
        [jnp.pad(top, ((0, 2), (0, 0))), jnp.pad(low, ((0, 0), (0, inner - low.shape[1])))]
    )
    count = 2 * t_count

    wide = width + N + LANES
    aligned = rows % TILE == 0
    size = lax.axis_size(SEQ)
    half = tokens // 2
    mine, tail = call(
        functools.partial(rows_kernel, sizes),
        "own_rows",
        (shape((half, model), BF16), shape((TILE, model), BF16)),
        [ints, hidden_in],
        [pltpu.SemaphoreType.DMA((2,))],
        fetch=True,
    )
    mine_b, mine_a = swap(mine, "b"), swap(mine, "a")
    inner_send = call(
        functools.partial(pack_kernel, heads),
        "pack_rows",
        shape((8, rows, wide + width), BF16),
        [inner_proj, small_proj, gate_proj],
        [
            *[pltpu.VMEM(x.shape, F32) for x in (inner_proj, small_proj, gate_proj)],
            pltpu.SemaphoreType.DMA((3,)),
        ],
        after=[mine],
        us=2,
        fetch=True,
    )
    inner_got = lax.all_to_all(inner_send, GROUP, 0, 0, tiled=True)

    if aligned:
        part, low, high, gate_part = call(
            repack_kernel,
            "repack_inner",
            (
                shape((8 * rows + TILE, width + N), BF16),
                shape((4 * rows, width + N), BF16),
                shape(((8 - 4) * rows + TILE, width + N), BF16),
                shape((8 * rows, width), BF16),
            ),
            [inner_got],
        )
        marks, inner_parts = [(0, 0, 0), (0, 1, 0)], [part, swap(part, "y")]
        for s in range(1, t_count):
            low, high = round_t(low, t_count), round_t(high, t_count)
            marks += [(s, 0, 0), (s, 0, 4), (s, 1, 0), (s, 1, 4)]
            inner_parts += [low, high, swap(low, "y"), swap(high, "y")]
        ready = [part]
    else:
        marks = None
        index = [stored_block(s, dy, p, info) for s in range(t_count) for dy in (0, 1) for p in range(8)]
        index = row_layout[jnp.stack(index)]
        inner_got = inner_got.reshape(8 * rows, wide + width)
        inner_weights = in_order(weight_parts(inner_got[:, :wide], t_count), index)
        gate_part = inner_got[:, wide:]
        ready = high = None

    halo0 = lax.ppermute(tail, SEQ, [(i, i + 1) for i in range(1, size - 1, 2)])
    halo1 = lax.ppermute(tail, SEQ, [(i, i + 2) for i in range(1, size - 2, 2)])

    over_b, over_a = call(
        functools.partial(forward_kernel, sizes),
        "forward_rows",
        (shape((half // 2, model), BF16), shape((half // 2 + TILE, model), BF16)),
        [ints, mine_b, mine_a, halo0, halo1],
        after=ready or [],
    )
    mine_d0, mine_d1 = swap(over_b, "b"), swap(over_a, "a")
    rows_in = [mine_b, mine_a, mine_d0, mine_d1]
    if aligned:
        gate_part = call(copy_kernel, "gate_part", shape(gate_part.shape, BF16), [gate_part], after=[high])
    gate_parts = weight_parts(gate_part, t_count)
    across = [(i, i ^ 3) for i in range(4)]
    out_rows = out_proj.shape[1]
    out_send = call(
        functools.partial(pack_out_kernel, sizes),
        "pack_out",
        [shape((out_rows, width), BF16)] * 4,
        [ints, out_proj.T],
        after=inner_parts[1:2] if aligned else [],
    )
    out_got = [
        out_send[0],
        swap(out_send[1], "b"),
        swap(out_send[2], "a"),
        lax.ppermute(out_send[3], ("a", "b"), across),
    ]
    out_part = call(join_kernel, "out_part", shape((4 * out_rows, width), BF16), out_got)
    out_parts = weight_parts(out_part, t_count)
    hidden = call(
        functools.partial(assemble_kernel, sizes),
        "assemble_rows",
        shape((2, TILE + 2 * tokens, model), BF16),
        [ints, hidden_in, *rows_in, *[swap(x, "tp") for x in rows_in], halo0, halo1],
        after=[],
        us=2,
    )
    if aligned:
        inner_weights = call(
            functools.partial(weights_kernel, sizes, marks, rows),
            "inner_weights",
            shape((model, wide), BF16),
            [ints, *inner_parts],
            us=15,
        )
    long = TILE + 2 * tokens
    raw, shared, step = call(
        inner_kernel,
        "inner_projection",
        (
            shape((2, long, width), BF16),
            shape((2, long, LANES), BF16),
            shape((2, long, LANES), F32),
        ),
        [hidden, inner_weights],
        us=3.5,
    )
    shared_other = swap(shared, "tp")
    init = lax.dynamic_slice_in_dim(init_states, me * heads, heads, 1)
    init = init.reshape(init.shape[0], width, N)
    chunks = 4 * tokens // PAGE
    x, b_in, c_in, cum, dt, ends, factors, summary = call(
        functools.partial(state_kernel, heads, tokens, sizes),
        "states",
        (
            shape((chunks, PAGE, width), BF16),
            shape((chunks, PAGE, N), BF16),
            shape((chunks, PAGE, N), BF16),
            shape((chunks, PAGE, LANES), F32),
            shape((chunks, PAGE, LANES), F32),
            shape((chunks, width, N), F32),
            shape((chunks, 8, N), F32),
            shape((2, width + 16, N), BF16),
        ),
        [ints, raw, shared, shared_other, step, params, init],
        after=gate_parts[2:3],
        us=7,
    )
    if aligned:
        gate_marks = [(s, dy, 0) for s in range(t_count) for dy in (0, 1)]
        gate_weights = call(
            functools.partial(weights_kernel, sizes, gate_marks, rows),
            "gate_weights",
            shape((model, width), BF16),
            [ints, *gate_parts],
            after=[summary],
            us=1,
        )
    else:
        gate_weights = in_order(gate_parts, index)
    if out_rows % TILE == 0:
        columns = call(
            functools.partial(columns_kernel, sizes, count, out_rows),
            "columns",
            shape((model, width), BF16),
            [ints, *out_parts],
            after=[summary],
            us=1,
        )
    else:
        index = [
            stored_block(s, dy, 2 * (me ^ rel), info) // 2
            for s in range(t_count)
            for dy in (0, 1)
            for rel in range(4)
        ]
        columns = in_order(out_parts, jnp.stack(index))
    theirs = swap(summary, "y")
    block = call(
        functools.partial(compose_kernel, heads, sizes),
        "compose",
        shape((width + 16, N), BF16),
        [ints, summary, theirs],
    )
    composed = block
    onward = [(i, i + 1) for i in range(t_count - 1)]
    block = lax.ppermute(block, "t", onward)
    entering = block
    if t_count > 2:
        total = block[:width].astype(F32).reshape(heads, head_dim, N)
        decay = block[width : width + heads, None, :].astype(F32)
        for _ in range(t_count - 2):
            block = lax.ppermute(block, "t", onward)
            total = total + decay * block[:width].astype(F32).reshape(heads, head_dim, N)
            decay = decay * block[width : width + heads, None, :].astype(F32)
        entering = total.reshape(width, N)
    y_within = call(
        functools.partial(within_kernel, heads, tokens, sizes),
        "within_chunks",
        shape((chunks, PAGE, width), F32),
        [ints, x, b_in, c_in, cum, dt, params, init],
        after=[composed, out_parts[2]],
        us=5,
    )
    states, *pages = call(
        functools.partial(enter_kernel, heads, tokens, sizes),
        "entering_states",
        (shape((chunks, width, N), BF16), *[shape((tokens // PAGE, width, N), BF16)] * 4),
        [ints, summary, theirs, entering, ends, factors],
        [pltpu.VMEM((2, width, N), F32)],
    )
    got_pages = [pages[0], swap(pages[1], "b"), swap(pages[2], "a"), lax.ppermute(pages[3], ("a", "b"), across)]
    gate = call(
        gate_kernel,
        "gate_projection",
        shape((2, long, width), BF16),
        [hidden, gate_weights],
        after=[states],
        us=2.5,
    )
    mixed, squares = call(
        functools.partial(finish_kernel, heads, tokens, sizes),
        "finish",
        (shape((chunks, PAGE, width), BF16), shape((chunks, 8, PAGE), F32)),
        [ints, states, c_in, cum, y_within, gate, params],
        after=got_pages[1:2],
        us=4,
    )

    dims = shape((4, PAGE + TILE, model), BF16)
    sent = call(functools.partial(mix_kernel, sizes, False), "mix_send", dims, [ints, mixed, squares, columns],
                after=got_pages[2:4], us=2.1)
    mix_sent = sent
    got = swap(sent, "tp")
    kept = call(functools.partial(mix_kernel, sizes, True), "mix_keep", dims, [ints, mixed, squares, columns],
                after=[mix_sent], us=2.1)
    mid = model // 2
    send_b, send_a, keep_b, keep_a = call(
        add_cores_kernel,
        "add_cores",
        (
            shape((2, PAGE + TILE, mid), BF16),
            shape((2, PAGE, mid), BF16),
            shape((2, PAGE + TILE, mid), F32),
            shape((2, PAGE, mid), F32),
        ),
        [kept, got],
    )
    per = tokens // PAGE
    state_pages = call(
        functools.partial(page_kernel, sizes), "pages", shape((per, 4, width, N), F32), [ints, *got_pages], after=[send_b], us=1.8
    )

    got_b, got_a = swap(send_b, "b"), swap(send_a, "a")
    send_a, send_b, left, right = call(
        add_second_kernel,
        "add_second",
        (
            shape((PAGE + TILE, mid), BF16),
            shape((PAGE, mid), BF16),
            shape((PAGE + TILE, mid), F32),
            shape((PAGE, mid), F32),
        ),
        [keep_b, got_b, keep_a, got_a],
    )
    got_left, got_right = swap(send_a, "a"), swap(send_b, "b")
    mixed_out = call(
        functools.partial(add_last_kernel, float(2 * inner)),
        "add_last",
        shape((PAGE, model), BF16),
        [left, got_left, right, got_right],
    )
    return (mixed_out, state_pages.reshape(per, half_heads, head_dim, N))


def solution(mesh):
    count = mesh.shape["seq"]
    fine = Mesh(mesh.devices.reshape(count // 8, 2, 2, 2, 2), SEQ + ("tp",))
    placed = (
        P(SEQ, None),
        P(SEQ + ("tp",), None),
        P(SEQ + ("tp",), None),
        P(SEQ + ("tp",), None),
        P(),
        P(None, "tp"),
        P(),
        P("tp"),
        P(),
        P("tp"),
        P("tp"),
        P("tp"),
        P("tp"),
        P("tp", SEQ),
        P(),
        P(),
        P(None, "tp", None, None),
        P(SEQ),
    )
    return jax.shard_map(
        on_device,
        mesh=fine,
        in_specs=placed,
        out_specs=(P(SEQ + ("tp",), None), P(SEQ, "tp", None, None)),
        check_vma=False,
    )
```

```python
import functools

import jax
import jax.numpy as jnp
from jax import lax
from jax.experimental import pallas as pl
from jax.experimental.pallas import tpu as pltpu
from jax.sharding import Mesh
from jax.sharding import PartitionSpec as P

N = 128
CONV = 4
PAGE = 128
TILE = 16
LANES = 128
EPSILON = 1e-05
F32 = jnp.float32
BF16 = jnp.bfloat16
HIGHEST = lax.Precision.HIGHEST
GROUP = ("a", "b", "tp")
SEQ = ("t", "a", "y", "b")
VMEM = pl.BlockSpec(memory_space=pltpu.VMEM)
SMEM = pl.BlockSpec(memory_space=pltpu.SMEM)
ANY = pl.BlockSpec(memory_space=pl.ANY)


def call(body, name, out_shape, ins, scratch=(), after=(), us=1.0, limit=16,
         fetch=False):
    specs = [SMEM if x.dtype == jnp.int32 else (ANY if fetch else VMEM) for x in ins]
    specs += [ANY] * len(after)
    first, last = len(ins), len(ins) + len(after)

    def kernel(*refs):
        body(*refs[:first], *refs[last:])

    return pl.pallas_call(
        kernel,
        name=name,
        out_shape=out_shape,
        in_specs=specs,
        out_specs=jax.tree.map(lambda _: VMEM, out_shape),
        scratch_shapes=list(scratch),
        cost_estimate=pl.CostEstimate(
            flops=int(us * 1e9), bytes_accessed=int(us * 3e6), transcendentals=0
        ),
        compiler_params=pltpu.CompilerParams(vmem_limit_bytes=limit << 20),
    )(*ins, *after)


def shape(dims, dtype):
    return jax.ShapeDtypeStruct(dims, dtype)


def dot(x, y, dims=((1,), (0,)), precision=None):
    return lax.dot_general(x, y, (dims, ((), ())), precision=precision, preferred_element_type=F32)


NT = ((1,), (1,))
TN = ((0,), (0,))


def swap(x, axis):
    return lax.ppermute(x, axis, [(0, 1), (1, 0)])


class Ints:
    def __init__(self, ref, at, size):
        self.ref, self.at, self.size = ref, at, size

    def __getitem__(self, k):
        return self.ref[self.at + k]


def views(ref, sizes):
    out, at = [], 0
    for size in sizes:
        out.append(Ints(ref, at, size))
        at += size
    return out


def stored_block(s, dy, place, info):
    t, y, count = info[3], info[4], info[5]
    a, b, c = place // 4, (place // 2) % 2, place % 2
    source = lax.rem(t - s + count, count)
    seq = ((source * 2 + a) * 2 + (y ^ dy)) * 2 + b
    return seq * 2 + c


def pack_kernel(heads, inner_hbm, small_hbm, gate_hbm, out, inner, small, gate, arrived):
    copies = [
        pltpu.make_async_copy(source, target, arrived.at[k])
        for k, (source, target) in enumerate(((inner_hbm, inner), (small_hbm, small), (gate_hbm, gate)))
    ]
    for copy in copies:
        copy.start()
    width = heads * 64
    rows = inner.shape[0]
    places = [(place, place % 2, place // 2) for place in range(8)]
    copies[0].wait()
    for place, c, group in places:
        at = (c * 4 + group) * width
        out[place, :, :width] = inner[:, at : at + width].astype(BF16)
    copies[1].wait()
    lane = lax.broadcasted_iota(jnp.int32, (rows, LANES), 1)
    steps = small[:, 2 * N :]
    steps = jnp.concatenate([steps, jnp.zeros((rows, LANES - steps.shape[1]), F32)], axis=1)
    for place, c, group in places:
        out[place, :, width : width + N] = small[:, c * N : (c + 1) * N].astype(BF16)
        first = (c * 4 + group) * heads
        moved = pltpu.roll(steps, LANES - first, 1) if first else steps
        out[place, :, width + N : width + N + LANES] = jnp.where(lane < heads, moved, 0.0).astype(BF16)
    copies[2].wait()
    for place, c, group in places:
        at = (c * 4 + group) * width
        out[place, :, width + N + LANES :] = gate[:, at : at + width].astype(BF16)


def rows_kernel(sizes, ints, hidden, mine, tail, arrived):
    c = views(ints, sizes)[0][1]
    half = mine.shape[0]
    at = pl.multiple_of(c * half, TILE)
    copies = (
        pltpu.make_async_copy(hidden.at[pl.ds(at, half), :], mine, arrived.at[0]),
        pltpu.make_async_copy(hidden.at[pl.ds(hidden.shape[0] - TILE, TILE), :], tail, arrived.at[1]),
    )
    for copy in copies:
        copy.start()
    for copy in copies:
        copy.wait()


def repack_kernel(got, whole, low, high, gate):
    rows, width = got.shape[1], whole.shape[1]
    cut = low.shape[0] // rows
    for place in range(8):
        gate[place * rows : (place + 1) * rows, :] = got[place, :, width + LANES :]
    lane = lax.broadcasted_iota(jnp.int32, (TILE, LANES), 1) // TILE
    for place in range(8):
        block = got[place, :, :width]
        whole[place * rows : (place + 1) * rows, :] = block
        half, at = (low, place) if place < cut else (high, place - cut)
        half[at * rows : (at + 1) * rows, :] = block
    for piece in range(rows // TILE):
        packed = jnp.zeros((TILE, LANES), F32)
        for place in range(8):
            steps = got[place, piece * TILE : (piece + 1) * TILE, width : width + LANES].astype(F32)
            steps = pltpu.roll(steps, place * TILE, 1) if place else steps
            packed = jnp.where(lane == place, steps, packed)
        here = slice(piece * LANES, (piece + 1) * LANES)
        whole[8 * rows :, here] = packed.astype(BF16)
        high[(8 - cut) * rows :, here] = packed.astype(BF16)
    rest = rows // TILE * LANES
    if rest < width:
        blank = jnp.zeros((TILE, width - rest), BF16)
        whole[8 * rows :, rest:] = blank
        high[(8 - cut) * rows :, rest:] = blank


def copy_kernel(source, out):
    out[...] = source[...]


def pack_out_kernel(sizes, ints, source, *outs):
    me = views(ints, sizes)[0][0]
    width = outs[0].shape[1]
    for rel, out in enumerate(outs):
        at = pl.multiple_of((me ^ rel) * width, LANES)
        out[...] = source[:, pl.ds(at, width)].astype(BF16)


def join_kernel(*refs):
    out, at = refs[-1], 0
    for source in refs[:-1]:
        out[at : at + source.shape[0], :] = source[...]
        at += source.shape[0]


def forward_kernel(sizes, ints, mine_b, mine_a, halo0, halo1, over_b, over_a):
    info = views(ints, sizes)[0]
    cut = over_b.shape[0]
    over_b[...] = mine_a[:cut, :]
    over_a[:cut, :] = mine_b[cut:, :]

    @pl.when(info[0] % 2 == 0)
    def _():
        over_a[cut:, :] = halo0[...]

    @pl.when(info[0] % 2 == 1)
    def _():
        over_a[cut:, :] = halo1[...]


def assemble_kernel(sizes, ints, own, mine_b, mine_a, mine_d0, mine_d1, other_b, other_a, other_d0,
                    other_d1, halo0, halo1, out):
    info = views(ints, sizes)[0]
    me, c = info[0], info[1]
    half = own.shape[0] // 2

    def put(q, h, row, source):
        at = TILE + ((q % 2) * 2 + h) * half + row
        out[q // 2, pl.ds(pl.multiple_of(at, TILE), source.shape[0]), :] = source

    put(me, 0, 0, own[:half, :])
    put(me, 1, 0, own[half:, :])
    for h, parts in ((c, (mine_b, mine_a, mine_d0, mine_d1)), (1 - c, (other_b, other_a, other_d0, other_d1))):
        cut = parts[2].shape[0]
        put(me ^ 1, h, 0, parts[0][...])
        put(me ^ 2, h, 0, parts[1][...])
        put(me ^ 3, h, 0, parts[2][...])
        put(me ^ 3, h, cut, parts[3][:cut, :])
    a = me // 2
    out[1 - a, :TILE, :] = mine_d1[cut:, :]

    @pl.when(me % 2 == 0)
    def _():
        out[a, :TILE, :] = halo0[...]

    @pl.when(me % 2 == 1)
    def _():
        out[a, :TILE, :] = halo1[...]


def place_parts(weights, marks, rows, parts, info, layout):
    width = parts[0].shape[1]
    lane = lax.broadcasted_iota(jnp.int32, (TILE, LANES), 1) // TILE
    for (s, dy, first), part in zip(marks, parts):
        count = part.shape[0] // rows
        for k in range(count):
            block = layout[stored_block(s, dy, first + k, info)]
            at = pl.multiple_of(block * rows, TILE)
            weights[pl.ds(at, rows), :width] = part[k * rows : (k + 1) * rows, :]
        base = count * rows
        if part.shape[0] == base:
            continue
        for place in range(8):
            block = layout[stored_block(s, dy, place, info)]
            for piece in range(rows // TILE):
                packed = part[base : base + TILE, piece * LANES : (piece + 1) * LANES]
                kept = jnp.where(lane == place, packed, jnp.zeros_like(packed))
                at = pl.multiple_of(block * rows + piece * TILE, TILE)
                weights[pl.ds(at, TILE), width:] = kept


def weights_kernel(sizes, marks, rows, *refs):
    info, layout = views(refs[0], sizes)[:2]
    place_parts(refs[1 + len(marks)], marks, rows, refs[1 : 1 + len(marks)], info, layout)


def inner_kernel(hidden, weights, raw_ref, shared_ref, step_ref):
    bc = raw_ref.shape[2]
    for run in range(2):
        result = dot(hidden[run], weights[:, bc:])
        shared_ref[run] = result[:, :LANES].astype(BF16)
        step = result[:, LANES:]
        for shift in (64, 32, 16):
            step = step + pltpu.roll(step, shift, 1)
        step_ref[run] = step
        raw_ref[run] = dot(hidden[run], weights[:, :bc]).astype(BF16)


def gate_kernel(hidden, weights, gate_ref):
    for run in range(2):
        gate_ref[run] = jax.nn.silu(dot(hidden[run], weights[...])).astype(BF16)


def starts_of(lengths):
    starts, total = [], jnp.int32(0)
    for k in range(lengths.size):
        starts.append(total)
        total = total + lengths[k]
    return starts


def head_lanes(row, heads, info):
    return pltpu.roll(row, lax.rem(LANES - info[0] * heads, LANES), 1)


def chunk_start(i, info, tokens):
    t, y = info[3], info[4]
    per = tokens // PAGE
    q = i // per
    seq = ((t * 2 + q // 2) * 2 + y) * 2 + q % 2
    return seq * tokens + (i % per) * PAGE


def last_start(position, starts):
    best = jnp.int32(0)
    for k in range(len(starts)):
        best = jnp.maximum(best, jnp.where(starts[k] <= position, starts[k], 0))
    return best


def first_positions(first, starts, dims):
    position = first + lax.broadcasted_iota(jnp.int32, dims, 0)
    best = jnp.zeros(dims, jnp.int32)
    for k in range(len(starts)):
        best = jnp.maximum(best, jnp.where(starts[k] <= position, starts[k], 0))
    return best


def conv_silu(window, taps, bias, offset):
    total = bias + taps[0:1, :] * window[TILE : TILE + PAGE]
    for lag in range(1, CONV):
        within = (offset >= lag).astype(F32)
        total = total + taps[lag : lag + 1, :] * window[TILE - lag : TILE - lag + PAGE] * within
    return total / (1.0 + jnp.exp(-total))


def pair_columns(values, pair):
    lane = lax.broadcasted_iota(jnp.int32, (PAGE, LANES), 1)
    left = values[:, 2 * pair : 2 * pair + 1]
    right = values[:, 2 * pair + 1 : 2 * pair + 2]
    return jnp.where(lane < 64, left, right)


def state_kernel(heads, tokens, sizes, ints, raw, own, other, step, params, init, x_ref, b_ref, c_ref,
                 cum_ref, dt_ref, end_ref, factor_ref, summary_ref):
    info, _, lengths, groups = views(ints, sizes)[:4]
    starts = starts_of(lengths)
    width = heads * 64
    here = pl.ds(pl.multiple_of(info[0] * width, LANES), width)
    taps, bias = params[0:4, here], params[4:5, here]
    taps2, bias2 = params[8:12, : 2 * N], params[12:13, : 2 * N]
    per_head = head_lanes(params[8:16, 2 * N : 2 * N + LANES], heads, info)
    dt_bias, rate = per_head[0:1], -jnp.exp(per_head[1:2])
    chunks = x_ref.shape[0]
    per_run = chunks // 2
    pairs = heads // 2
    row = lax.broadcasted_iota(jnp.int32, (PAGE, PAGE), 0)
    col = lax.broadcasted_iota(jnp.int32, (PAGE, PAGE), 1)
    below = (row >= col).astype(F32)

    def one(i, carry):
        first = chunk_start(i, info, tokens)
        opened = last_start(first + PAGE - 1, starts)
        alive = (opened < first).astype(F32)
        start_of = first_positions(first, starts, (PAGE, 1))
        offset = first + lax.broadcasted_iota(jnp.int32, (PAGE, 1), 0) - start_of
        q = i // per_run
        at = pl.multiple_of((i % per_run) * PAGE, TILE)
        window = pl.ds(at, PAGE + TILE)
        x = conv_silu(raw[q, window, :].astype(F32), taps, bias, offset)
        is_first = info[1] == 0
        mine, theirs = own[q, window, :].astype(F32), other[q, window, :].astype(F32)
        b_raw = jnp.where(is_first, mine, theirs)
        c_raw = jnp.where(is_first, theirs, mine)
        b = conv_silu(b_raw, taps2[:, :LANES], bias2[:, :LANES], offset).astype(BF16)
        c = conv_silu(c_raw, taps2[:, LANES:], bias2[:, LANES:], offset).astype(BF16)
        raw_step = step[q, pl.ds(pl.multiple_of(at + TILE, TILE), PAGE), :]
        v = raw_step + dt_bias
        dt = jnp.maximum(v, 0.0) + jnp.log1p(jnp.exp(-jnp.abs(v)))
        log_rate = rate * dt
        cum = dot(below, log_rate, precision=HIGHEST)
        last = cum[PAGE - 1 : PAGE, :]
        kept = (row >= opened - first).astype(F32)
        weight = jnp.exp(last - cum) * dt * kept
        cum_t = cum.T
        x_ref[i] = x.astype(BF16)
        b_ref[i] = b
        c_ref[i] = c
        cum_ref[i] = cum
        dt_ref[i] = dt
        last_t = cum_t[0:8, PAGE - 1 : PAGE]
        factor_ref[i] = jnp.broadcast_to(jnp.exp(last_t), (8, LANES)) * alive
        for pair in range(pairs):
            here = slice(pair * LANES, (pair + 1) * LANES)
            scaled = (x[:, here] * pair_columns(weight, pair)).astype(BF16)
            end_ref[i, here, :] = dot(scaled, b, TN)

        @pl.when(opened >= first)
        def _():
            for k in range(len(starts)):

                @pl.when(starts[k] == opened)
                def _():
                    at_start = col == opened - first - 1
                    before = jnp.sum(jnp.where(at_start, cum_t, 0.0), axis=1, keepdims=True)
                    opening = jnp.broadcast_to(jnp.exp(last_t - before[0:8]), (8, LANES))
                    for h in range(heads):
                        here = slice(h * 64, (h + 1) * 64)
                        entered = opening[h : h + 1, :] * init[groups[k], here, :]
                        end_ref[i, here, :] = end_ref[i, here, :] + entered

        return carry

    lax.fori_loop(0, chunks, one, 0, unroll=2)
    for run in range(2):
        factor = factor_ref[run * per_run]
        for i in range(run * per_run + 1, (run + 1) * per_run):
            for h in range(heads):
                here = slice(h * 64, (h + 1) * 64)
                end_ref[i, here, :] = end_ref[i, here, :] + factor_ref[i, h : h + 1, :] * end_ref[i - 1, here, :]
            factor = factor * factor_ref[i]
            factor_ref[i] = factor
        summary_ref[run, : heads * 64, :] = end_ref[(run + 1) * per_run - 1].astype(BF16)
        tail = jnp.concatenate([factor, jnp.zeros_like(factor)], axis=0)
        summary_ref[run, heads * 64 :, :] = tail.astype(BF16)


def within_kernel(heads, tokens, sizes, ints, x_ref, b_ref, c_ref, cum_ref, dt_ref, params, init, y_ref):
    info, _, lengths, groups = views(ints, sizes)[:4]
    starts = starts_of(lengths)
    skip = head_lanes(params[8:16, 2 * N : 2 * N + LANES], heads, info)[2:3]
    skip = jnp.broadcast_to(skip, (PAGE, LANES))
    chunks = x_ref.shape[0]
    pairs = heads // 2
    row = lax.broadcasted_iota(jnp.int32, (PAGE, PAGE), 0)
    col = lax.broadcasted_iota(jnp.int32, (PAGE, PAGE), 1)
    lane = lax.broadcasted_iota(jnp.int32, (PAGE, LANES), 1)

    def one(i, carry):
        first = chunk_start(i, info, tokens)
        start_of = first_positions(first, starts, (PAGE, PAGE))
        bias = jnp.where((row >= col) & (col >= start_of - first), 0.0, -1e30)
        b, c = b_ref[i], c_ref[i]
        cum, dt = cum_ref[i], dt_ref[i]
        cum_t = cum.T
        scores = dot(c, b, NT)
        for pair in range(pairs):
            here = slice(pair * LANES, (pair + 1) * LANES)
            x = x_ref[i, :, here].astype(F32)
            scaled = x * pair_columns(dt, pair)
            mixing = []
            for h in (2 * pair, 2 * pair + 1):
                gap = cum[:, h : h + 1] + bias - cum_t[h : h + 1, :]
                mixing.append((scores * jnp.exp(gap)).astype(BF16))
            both = jnp.concatenate(
                [jnp.where(lane < 64, scaled, 0.0), jnp.where(lane < 64, 0.0, scaled)], axis=0
            ).astype(BF16)
            y = dot(jnp.concatenate(mixing, axis=1), both)
            y_ref[i, :, here] = y + pair_columns(skip, pair) * x
        @pl.when(last_start(first + PAGE - 1, starts) >= first)
        def _():
            for k in range(len(starts)):
                start = starts[k]

                @pl.when((start >= first) & (start < first + PAGE))
                def _():
                    at_start = row == start - first - 1
                    before = jnp.sum(jnp.where(at_start, cum, 0.0), axis=0, keepdims=True)
                    opening = jnp.exp(jnp.minimum(cum - before, 0.0))
                    opening = jnp.where(start_of == start, opening, 0.0)
                    for pair in range(pairs):
                        here = slice(pair * LANES, (pair + 1) * LANES)
                        read = dot(c, init[groups[k], here, :].astype(BF16), NT)
                        y_ref[i, :, here] = y_ref[i, :, here] + pair_columns(opening, pair) * read

        return carry

    lax.fori_loop(0, chunks, one, 0, unroll=2)


def onto(run, h, before):
    here = slice(h * 64, (h + 1) * 64)
    decay = run[run.shape[0] - 16 + h : run.shape[0] - 16 + h + 1, :].astype(F32)
    return decay * before + run[here, :].astype(F32)


def compose_kernel(heads, sizes, ints, mine, theirs, block_ref):
    info = views(ints, sizes)[0]
    low = info[4] == 0
    runs = []
    for a in range(2):
        m, q = mine[a].astype(F32), theirs[a].astype(F32)
        runs += [jnp.where(low, m, q), jnp.where(low, q, m)]
    total = runs[0]
    for run in runs[1:]:
        parts = []
        for h in range(heads):
            parts.append(onto(run, h, total[h * 64 : (h + 1) * 64, :]))
        tail = total[heads * 64 :, :] * run[heads * 64 :, :]
        total = jnp.concatenate(parts + [tail], axis=0)
    block_ref[...] = total.astype(BF16)


def enter_kernel(heads, tokens, sizes, ints, mine, theirs, entering, end_ref, factor_ref, states,
                 page0, page1, page2, page3, starting):
    info = views(ints, sizes)[0]
    me, y = info[0], info[4]
    per = tokens // PAGE
    per_run = states.shape[0] // 2
    for h in range(heads):
        here = slice(h * 64, (h + 1) * 64)
        outside = entering[here, :].astype(F32)
        first = jnp.where(y == 0, outside, onto(theirs[0], h, outside))
        starting[0, here, :] = first
        second = onto(mine[0], h, first)
        third = jnp.where(y == 0, onto(theirs[0], h, second), onto(theirs[1], h, second))
        starting[1, here, :] = third
    states[0] = starting[0].astype(BF16)
    states[per_run] = starting[1].astype(BF16)
    for rel, page in enumerate((page0, page1, page2, page3)):
        for k in range(per):
            i = (me ^ rel) * per + k
            run = i // per_run
            for h in range(heads):
                here = slice(h * 64, (h + 1) * 64)
                after = end_ref[i, here, :] + factor_ref[i, h : h + 1, :] * starting[run, here, :]
                page[k, here, :] = after.astype(BF16)

            @pl.when(i % per_run < per_run - 1)
            def _():
                states[i + 1] = page[k]


def finish_kernel(heads, tokens, sizes, ints, states, c_ref, cum_ref, y_ref, gate, params, mixed_ref,
                  square_ref):
    info, _, lengths = views(ints, sizes)[:3]
    starts = starts_of(lengths)
    width = heads * 64
    gain = params[5:6, pl.ds(pl.multiple_of(info[0] * width, LANES), width)]
    chunks = c_ref.shape[0]
    per_run = chunks // 2
    pairs = heads // 2
    ones = jnp.ones((8, LANES), F32)

    def one(i, carry):
        run = i // per_run
        first = chunk_start(i, info, tokens)
        alive = (first_positions(first, starts, (PAGE, LANES)) < first).astype(F32)
        decay = jnp.exp(cum_ref[i]) * alive
        read = dot(c_ref[i], states[i], NT)
        rows = pl.ds(pl.multiple_of(TILE + (i % per_run) * PAGE, TILE), PAGE)
        squares = jnp.zeros((PAGE, LANES), F32)
        for pair in range(pairs):
            here = slice(pair * LANES, (pair + 1) * LANES)
            value = y_ref[i, :, here] + pair_columns(decay, pair) * read[:, here]
            value = value * gate[run, rows, here].astype(F32)
            mixed_ref[i, :, here] = (value * gain[:, here]).astype(BF16)
            squares = squares + value * value
        square_ref[i] = dot(ones, squares, NT, HIGHEST)
        return carry

    lax.fori_loop(0, chunks, one, 0, unroll=2)


def columns_kernel(sizes, count, rows, ints, *refs):
    info = views(ints, sizes)[0]
    parts, out = refs[:count], refs[count]
    for index, part in enumerate(parts):
        for rel in range(4):
            seq = stored_block(index // 2, index % 2, 2 * (info[0] ^ rel), info) // 2
            at = pl.multiple_of(seq * rows, TILE)
            out[pl.ds(at, rows), :] = part[rel * rows : (rel + 1) * rows, :]


def mix_kernel(sizes, keep, ints, mixed, squares, columns, out):
    info = views(ints, sizes)[0]
    me, c = info[0], info[1]
    half = c if keep else 1 - c
    for rel in range(4):
        i = (me ^ rel) * 2 + half
        out[rel, :PAGE, :] = dot(mixed[i], columns[...], NT).astype(BF16)
        both = jnp.concatenate([squares[i], squares[i]], axis=0)
        out[rel, PAGE:, :LANES] = both.astype(BF16)
        out[rel, PAGE:, LANES:] = jnp.zeros((TILE, out.shape[2] - LANES), BF16)


def add_cores_kernel(kept, got, send_b, send_a, keep_b, keep_a):
    mid = send_b.shape[2]
    for k in (0, 1):
        total = kept[2 * k + 1, :, :mid].astype(F32) + got[2 * k + 1, :, :mid].astype(F32)
        send_b[k] = total.astype(BF16)
        keep_b[k] = kept[2 * k, :, :mid].astype(F32) + got[2 * k, :, :mid].astype(F32)
        total = kept[k + 2, :PAGE, mid:].astype(F32) + got[k + 2, :PAGE, mid:].astype(F32)
        send_a[k] = total.astype(BF16)
        keep_a[k] = kept[k, :PAGE, mid:].astype(F32) + got[k, :PAGE, mid:].astype(F32)


def add_second_kernel(keep_b, got_b, keep_a, got_a, send_a, send_b, left, right):
    send_a[...] = (keep_b[1] + got_b[1].astype(F32)).astype(BF16)
    left[...] = keep_b[0] + got_b[0].astype(F32)
    send_b[...] = (keep_a[1] + got_a[1].astype(F32)).astype(BF16)
    right[...] = keep_a[0] + got_a[0].astype(F32)


def add_last_kernel(channels, left, got_left, right, got_right, out):
    mid = left.shape[1]
    squares = left[PAGE : PAGE + 1, :LANES] + got_left[PAGE:, :LANES].astype(F32)[0:1]
    row = lax.broadcasted_iota(jnp.int32, (PAGE, PAGE), 0)
    col = lax.broadcasted_iota(jnp.int32, (PAGE, PAGE), 1)
    squares = jnp.sum(jnp.where(row == col, squares, 0.0), axis=1, keepdims=True)
    scale = lax.rsqrt(squares / channels + EPSILON)
    out[:, :mid] = ((left[:PAGE] + got_left[:PAGE, :].astype(F32)) * scale).astype(BF16)
    out[:, mid:] = ((right[...] + got_right[...].astype(F32)) * scale).astype(BF16)


def page_kernel(sizes, ints, own, from_b, from_a, from_d, out):
    info, _, _, _, table = views(ints, sizes)
    me, seq, per = info[0], info[6], own.shape[0]
    for k in range(per):
        slot = table[k] - seq * per
        for rel, source in enumerate((own, from_b, from_a, from_d)):
            out[slot, me ^ rel] = source[k].astype(F32)


def round_t(x, count):
    return lax.ppermute(x, "t", [(i, (i + 1) % count) for i in range(count)])


def weight_parts(part, count):
    parts = []
    for s in range(count):
        part = round_t(part, count) if s > 0 else part
        parts += [part, swap(part, "y")]
    return parts


def in_order(parts, index):
    stacked = jnp.stack(parts)
    blocks = stacked.reshape((-1, stacked.shape[1] * len(parts) // index.shape[0], stacked.shape[2]))
    return jnp.zeros_like(blocks).at[index].set(blocks).reshape(-1, stacked.shape[2])


def on_device(
    hidden_in,
    gate_proj,
    inner_proj,
    small_proj,
    row_layout,
    conv_inner,
    conv_shared,
    bias_inner,
    bias_shared,
    dt_bias,
    decay_log,
    skip_gain,
    norm_gain,
    out_proj,
    prompt_lengths,
    group_map,
    init_states,
    page_table,
):
    tokens, model = hidden_in.shape
    rows = gate_proj.shape[0]
    half_heads = dt_bias.shape[0]
    heads = half_heads // 4
    inner = conv_inner.shape[1]
    head_dim = inner // half_heads
    width = heads * head_dim
    t_count = lax.axis_size("t")
    t, a, y, b, c = (lax.axis_index(name) for name in ("t", "a", "y", "b", "tp"))
    me = a * 2 + b
    seq = ((t * 2 + a) * 2 + y) * 2 + b
    info = jnp.stack([me, c, 0 * c, t, y, 0 * c + t_count, seq, 0 * c]).astype(jnp.int32)
    pieces = [info, row_layout, prompt_lengths, group_map, page_table]
    sizes = tuple(piece.shape[0] for piece in pieces)
    ints = jnp.concatenate(pieces)
    per_head = jnp.pad(jnp.stack([dt_bias, decay_log, skip_gain]), ((0, 5), (0, LANES - half_heads)))
    top = jnp.concatenate([conv_inner, bias_inner[None], norm_gain[None]])
    low = jnp.concatenate([conv_shared, bias_shared[None]])
    low = jnp.concatenate([jnp.pad(low, ((0, 3), (0, 0))), per_head], axis=1)
    params = jnp.concatenate(
        [jnp.pad(top, ((0, 2), (0, 0))), jnp.pad(low, ((0, 0), (0, inner - low.shape[1])))]
    )
    count = 2 * t_count

    wide = width + N + LANES
    aligned = rows % TILE == 0
    size = lax.axis_size(SEQ)
    half = tokens // 2
    inner_send = call(
        functools.partial(pack_kernel, heads),
        "pack_rows",
        shape((8, rows, wide + width), BF16),
        [inner_proj, small_proj, gate_proj],
        [
            *[pltpu.VMEM(x.shape, F32) for x in (inner_proj, small_proj, gate_proj)],
            pltpu.SemaphoreType.DMA((3,)),
        ],
        us=2,
        limit=56,
        fetch=True,
    )
    inner_got = lax.all_to_all(inner_send, GROUP, 0, 0, tiled=True)
    mine, tail = call(
        functools.partial(rows_kernel, sizes),
        "own_rows",
        (shape((half, model), BF16), shape((TILE, model), BF16)),
        [ints, hidden_in],
        [pltpu.SemaphoreType.DMA((2,))],
        after=[inner_send],
        limit=56,
        fetch=True,
    )
    mine_b, mine_a = swap(mine, "b"), swap(mine, "a")

    if aligned:
        part, low, high, gate_part = call(
            repack_kernel,
            "repack_inner",
            (
                shape((8 * rows + TILE, width + N), BF16),
                shape((5 * rows, width + N), BF16),
                shape(((8 - 5) * rows + TILE, width + N), BF16),
                shape((8 * rows, width), BF16),
            ),
            [inner_got],
        )
        marks, inner_parts = [(0, 0, 0), (0, 1, 0)], [part, swap(part, "y")]
        for s in range(1, t_count):
            low, high = round_t(low, t_count), round_t(high, t_count)
            marks += [(s, 0, 0), (s, 0, 5), (s, 1, 0), (s, 1, 5)]
            inner_parts += [low, high, swap(low, "y"), swap(high, "y")]
        ready = [part]
    else:
        marks = None
        index = [stored_block(s, dy, p, info) for s in range(t_count) for dy in (0, 1) for p in range(8)]
        index = row_layout[jnp.stack(index)]
        inner_got = inner_got.reshape(8 * rows, wide + width)
        inner_weights = in_order(weight_parts(inner_got[:, :wide], t_count), index)
        gate_part = inner_got[:, wide:]
        ready = high = None

    halo0 = lax.ppermute(tail, SEQ, [(i, i + 1) for i in range(1, size - 1, 2)])
    halo1 = lax.ppermute(tail, SEQ, [(i, i + 2) for i in range(1, size - 2, 2)])

    over_b, over_a = call(
        functools.partial(forward_kernel, sizes),
        "forward_rows",
        (shape((half // 2, model), BF16), shape((half // 2 + TILE, model), BF16)),
        [ints, mine_b, mine_a, halo0, halo1],
        after=ready or [],
    )
    mine_d0, mine_d1 = swap(over_b, "b"), swap(over_a, "a")
    rows_in = [mine_b, mine_a, mine_d0, mine_d1]
    if aligned:
        gate_part = call(copy_kernel, "gate_part", shape(gate_part.shape, BF16), [gate_part], after=[high])
    gate_parts = weight_parts(gate_part, t_count)
    across = [(i, i ^ 3) for i in range(4)]
    out_rows = out_proj.shape[1]
    out_send = call(
        functools.partial(pack_out_kernel, sizes),
        "pack_out",
        [shape((out_rows, width), BF16)] * 4,
        [ints, out_proj.T],
        after=inner_parts[1:2] if aligned else [],
    )
    out_got = [
        out_send[0],
        swap(out_send[1], "b"),
        swap(out_send[2], "a"),
        lax.ppermute(out_send[3], ("a", "b"), across),
    ]
    out_part = call(join_kernel, "out_part", shape((4 * out_rows, width), BF16), out_got)
    out_parts = weight_parts(out_part, t_count)
    hidden = call(
        functools.partial(assemble_kernel, sizes),
        "assemble_rows",
        shape((2, TILE + 2 * tokens, model), BF16),
        [ints, hidden_in, *rows_in, *[swap(x, "tp") for x in rows_in], halo0, halo1],
        after=[],
        us=2,
    )
    if aligned:
        inner_weights = call(
            functools.partial(weights_kernel, sizes, marks, rows),
            "inner_weights",
            shape((model, wide), BF16),
            [ints, *inner_parts],
            us=15,
        )
    long = TILE + 2 * tokens
    raw, shared, step = call(
        inner_kernel,
        "inner_projection",
        (
            shape((2, long, width), BF16),
            shape((2, long, LANES), BF16),
            shape((2, long, LANES), F32),
        ),
        [hidden, inner_weights],
        us=3.5,
    )
    shared_other = swap(shared, "tp")
    init = lax.dynamic_slice_in_dim(init_states, me * heads, heads, 1)
    init = init.reshape(init.shape[0], width, N)
    chunks = 4 * tokens // PAGE
    x, b_in, c_in, cum, dt, ends, factors, summary = call(
        functools.partial(state_kernel, heads, tokens, sizes),
        "states",
        (
            shape((chunks, PAGE, width), BF16),
            shape((chunks, PAGE, N), BF16),
            shape((chunks, PAGE, N), BF16),
            shape((chunks, PAGE, LANES), F32),
            shape((chunks, PAGE, LANES), F32),
            shape((chunks, width, N), F32),
            shape((chunks, 8, N), F32),
            shape((2, width + 16, N), BF16),
        ),
        [ints, raw, shared, shared_other, step, params, init],
        after=gate_parts[2:3],
        us=7,
    )
    if aligned:
        gate_marks = [(s, dy, 0) for s in range(t_count) for dy in (0, 1)]
        gate_weights = call(
            functools.partial(weights_kernel, sizes, gate_marks, rows),
            "gate_weights",
            shape((model, width), BF16),
            [ints, *gate_parts],
            after=[summary],
            us=1,
        )
    else:
        gate_weights = in_order(gate_parts, index)
    if out_rows % TILE == 0:
        columns = call(
            functools.partial(columns_kernel, sizes, count, out_rows),
            "columns",
            shape((model, width), BF16),
            [ints, *out_parts],
            after=[summary],
            us=1,
        )
    else:
        index = [
            stored_block(s, dy, 2 * (me ^ rel), info) // 2
            for s in range(t_count)
            for dy in (0, 1)
            for rel in range(4)
        ]
        columns = in_order(out_parts, jnp.stack(index))
    theirs = swap(summary, "y")
    block = call(
        functools.partial(compose_kernel, heads, sizes),
        "compose",
        shape((width + 16, N), BF16),
        [ints, summary, theirs],
    )
    composed = block
    onward = [(i, i + 1) for i in range(t_count - 1)]
    block = lax.ppermute(block, "t", onward)
    entering = block
    if t_count > 2:
        total = block[:width].astype(F32).reshape(heads, head_dim, N)
        decay = block[width : width + heads, None, :].astype(F32)
        for _ in range(t_count - 2):
            block = lax.ppermute(block, "t", onward)
            total = total + decay * block[:width].astype(F32).reshape(heads, head_dim, N)
            decay = decay * block[width : width + heads, None, :].astype(F32)
        entering = total.reshape(width, N)
    y_within = call(
        functools.partial(within_kernel, heads, tokens, sizes),
        "within_chunks",
        shape((chunks, PAGE, width), F32),
        [ints, x, b_in, c_in, cum, dt, params, init],
        after=[composed, out_parts[2]],
        us=5,
    )
    states, *pages = call(
        functools.partial(enter_kernel, heads, tokens, sizes),
        "entering_states",
        (shape((chunks, width, N), BF16), *[shape((tokens // PAGE, width, N), BF16)] * 4),
        [ints, summary, theirs, entering, ends, factors],
        [pltpu.VMEM((2, width, N), F32)],
    )
    got_pages = [pages[0], swap(pages[1], "b"), swap(pages[2], "a"), lax.ppermute(pages[3], ("a", "b"), across)]
    gate = call(
        gate_kernel,
        "gate_projection",
        shape((2, long, width), BF16),
        [hidden, gate_weights],
        after=[states],
        us=2.5,
    )
    mixed, squares = call(
        functools.partial(finish_kernel, heads, tokens, sizes),
        "finish",
        (shape((chunks, PAGE, width), BF16), shape((chunks, 8, PAGE), F32)),
        [ints, states, c_in, cum, y_within, gate, params],
        after=got_pages[1:2],
        us=4,
    )

    dims = shape((4, PAGE + TILE, model), BF16)
    sent = call(functools.partial(mix_kernel, sizes, False), "mix_send", dims, [ints, mixed, squares, columns],
                after=got_pages[2:4], us=2.1)
    mix_sent = sent
    got = swap(sent, "tp")
    kept = call(functools.partial(mix_kernel, sizes, True), "mix_keep", dims, [ints, mixed, squares, columns],
                after=[mix_sent], us=2.1)
    mid = model // 2
    send_b, send_a, keep_b, keep_a = call(
        add_cores_kernel,
        "add_cores",
        (
            shape((2, PAGE + TILE, mid), BF16),
            shape((2, PAGE, mid), BF16),
            shape((2, PAGE + TILE, mid), F32),
            shape((2, PAGE, mid), F32),
        ),
        [kept, got],
    )
    per = tokens // PAGE
    state_pages = call(
        functools.partial(page_kernel, sizes), "pages", shape((per, 4, width, N), F32), [ints, *got_pages], after=[send_b], us=1.8
    )

    got_b, got_a = swap(send_b, "b"), swap(send_a, "a")
    send_a, send_b, left, right = call(
        add_second_kernel,
        "add_second",
        (
            shape((PAGE + TILE, mid), BF16),
            shape((PAGE, mid), BF16),
            shape((PAGE + TILE, mid), F32),
            shape((PAGE, mid), F32),
        ),
        [keep_b, got_b, keep_a, got_a],
    )
    got_left, got_right = swap(send_a, "a"), swap(send_b, "b")
    mixed_out = call(
        functools.partial(add_last_kernel, float(2 * inner)),
        "add_last",
        shape((PAGE, model), BF16),
        [left, got_left, right, got_right],
    )
    return (mixed_out, state_pages.reshape(per, half_heads, head_dim, N))


def solution(mesh):
    count = mesh.shape["seq"]
    fine = Mesh(mesh.devices.reshape(count // 8, 2, 2, 2, 2), SEQ + ("tp",))
    placed = (
        P(SEQ, None),
        P(SEQ + ("tp",), None),
        P(SEQ + ("tp",), None),
        P(SEQ + ("tp",), None),
        P(),
        P(None, "tp"),
        P(),
        P("tp"),
        P(),
        P("tp"),
        P("tp"),
        P("tp"),
        P("tp"),
        P("tp", SEQ),
        P(),
        P(),
        P(None, "tp", None, None),
        P(SEQ),
    )
    return jax.shard_map(
        on_device,
        mesh=fine,
        in_specs=placed,
        out_specs=(P(SEQ + ("tp",), None), P(SEQ, "tp", None, None)),
        check_vma=False,
    )
```

```python
import functools

import jax
import jax.numpy as jnp
from jax import lax
from jax.experimental import pallas as pl
from jax.experimental.pallas import tpu as pltpu
from jax.sharding import Mesh
from jax.sharding import PartitionSpec as P

N = 128
CONV = 4
PAGE = 128
TILE = 16
LANES = 128
EPSILON = 1e-05
F32 = jnp.float32
BF16 = jnp.bfloat16
HIGHEST = lax.Precision.HIGHEST
GROUP = ("a", "b", "tp")
SEQ = ("t", "a", "y", "b")
VMEM = pl.BlockSpec(memory_space=pltpu.VMEM)
SMEM = pl.BlockSpec(memory_space=pltpu.SMEM)
ANY = pl.BlockSpec(memory_space=pl.ANY)


def call(body, name, out_shape, ins, scratch=(), after=(), us=1.0, limit=16,
         fetch=False):
    specs = [SMEM if x.dtype == jnp.int32 else (ANY if fetch else VMEM) for x in ins]
    specs += [ANY] * len(after)
    first, last = len(ins), len(ins) + len(after)

    def kernel(*refs):
        body(*refs[:first], *refs[last:])

    return pl.pallas_call(
        kernel,
        name=name,
        out_shape=out_shape,
        in_specs=specs,
        out_specs=jax.tree.map(lambda _: VMEM, out_shape),
        scratch_shapes=list(scratch),
        cost_estimate=pl.CostEstimate(
            flops=int(us * 1e9), bytes_accessed=int(us * 3e6), transcendentals=0
        ),
        compiler_params=pltpu.CompilerParams(vmem_limit_bytes=limit << 20),
    )(*ins, *after)


def shape(dims, dtype):
    return jax.ShapeDtypeStruct(dims, dtype)


def dot(x, y, dims=((1,), (0,)), precision=None):
    return lax.dot_general(x, y, (dims, ((), ())), precision=precision, preferred_element_type=F32)


NT = ((1,), (1,))
TN = ((0,), (0,))


def swap(x, axis):
    return lax.ppermute(x, axis, [(0, 1), (1, 0)])


class Ints:
    def __init__(self, ref, at, size):
        self.ref, self.at, self.size = ref, at, size

    def __getitem__(self, k):
        return self.ref[self.at + k]


def views(ref, sizes):
    out, at = [], 0
    for size in sizes:
        out.append(Ints(ref, at, size))
        at += size
    return out


def stored_block(s, dy, place, info):
    t, y, count = info[3], info[4], info[5]
    a, b, c = place // 4, (place // 2) % 2, place % 2
    source = lax.rem(t - s + count, count)
    seq = ((source * 2 + a) * 2 + (y ^ dy)) * 2 + b
    return seq * 2 + c


def pack_kernel(heads, inner_hbm, small_hbm, gate_hbm, out, inner, small, gate, arrived):
    copies = [
        pltpu.make_async_copy(source, target, arrived.at[k])
        for k, (source, target) in enumerate(((inner_hbm, inner), (small_hbm, small), (gate_hbm, gate)))
    ]
    for copy in copies:
        copy.start()
    width = heads * 64
    rows = inner.shape[0]
    places = [(place, place % 2, place // 2) for place in range(8)]
    copies[0].wait()
    for place, c, group in places:
        at = (c * 4 + group) * width
        out[place, :, :width] = inner[:, at : at + width].astype(BF16)
    copies[1].wait()
    lane = lax.broadcasted_iota(jnp.int32, (rows, LANES), 1)
    steps = small[:, 2 * N :]
    steps = jnp.concatenate([steps, jnp.zeros((rows, LANES - steps.shape[1]), F32)], axis=1)
    for place, c, group in places:
        out[place, :, width : width + N] = small[:, c * N : (c + 1) * N].astype(BF16)
        first = (c * 4 + group) * heads
        moved = pltpu.roll(steps, LANES - first, 1) if first else steps
        out[place, :, width + N : width + N + LANES] = jnp.where(lane < heads, moved, 0.0).astype(BF16)
    copies[2].wait()
    for place, c, group in places:
        at = (c * 4 + group) * width
        out[place, :, width + N + LANES :] = gate[:, at : at + width].astype(BF16)


def rows_kernel(sizes, ints, hidden, mine, tail, arrived):
    c = views(ints, sizes)[0][1]
    half = mine.shape[0]
    at = pl.multiple_of(c * half, TILE)
    copies = (
        pltpu.make_async_copy(hidden.at[pl.ds(at, half), :], mine, arrived.at[0]),
        pltpu.make_async_copy(hidden.at[pl.ds(hidden.shape[0] - TILE, TILE), :], tail, arrived.at[1]),
    )
    for copy in copies:
        copy.start()
    for copy in copies:
        copy.wait()


def repack_kernel(got, whole, low, high, gate):
    rows, width = got.shape[1], whole.shape[1]
    cut = low.shape[0] // rows
    for place in range(8):
        gate[place * rows : (place + 1) * rows, :] = got[place, :, width + LANES :]
    lane = lax.broadcasted_iota(jnp.int32, (TILE, LANES), 1) // TILE
    for place in range(8):
        block = got[place, :, :width]
        whole[place * rows : (place + 1) * rows, :] = block
        half, at = (low, place) if place < cut else (high, place - cut)
        half[at * rows : (at + 1) * rows, :] = block
    for piece in range(rows // TILE):
        packed = jnp.zeros((TILE, LANES), F32)
        for place in range(8):
            steps = got[place, piece * TILE : (piece + 1) * TILE, width : width + LANES].astype(F32)
            steps = pltpu.roll(steps, place * TILE, 1) if place else steps
            packed = jnp.where(lane == place, steps, packed)
        here = slice(piece * LANES, (piece + 1) * LANES)
        whole[8 * rows :, here] = packed.astype(BF16)
        high[(8 - cut) * rows :, here] = packed.astype(BF16)
    rest = rows // TILE * LANES
    if rest < width:
        blank = jnp.zeros((TILE, width - rest), BF16)
        whole[8 * rows :, rest:] = blank
        high[(8 - cut) * rows :, rest:] = blank


def copy_kernel(source, out):
    out[...] = source[...]


def pack_out_kernel(sizes, ints, source, *outs):
    me = views(ints, sizes)[0][0]
    width = outs[0].shape[1]
    for rel, out in enumerate(outs):
        at = pl.multiple_of((me ^ rel) * width, LANES)
        out[...] = source[:, pl.ds(at, width)].astype(BF16)


def join_kernel(*refs):
    out, at = refs[-1], 0
    for source in refs[:-1]:
        out[at : at + source.shape[0], :] = source[...]
        at += source.shape[0]


def forward_kernel(sizes, ints, mine_b, mine_a, halo0, halo1, over_b, over_a):
    info = views(ints, sizes)[0]
    cut = over_b.shape[0]
    over_b[...] = mine_a[:cut, :]
    over_a[:cut, :] = mine_b[cut:, :]

    @pl.when(info[0] % 2 == 0)
    def _():
        over_a[cut:, :] = halo0[...]

    @pl.when(info[0] % 2 == 1)
    def _():
        over_a[cut:, :] = halo1[...]


def assemble_kernel(sizes, ints, own, mine_b, mine_a, mine_d0, mine_d1, other_b, other_a, other_d0,
                    other_d1, halo0, halo1, out):
    info = views(ints, sizes)[0]
    me, c = info[0], info[1]
    half = own.shape[0] // 2

    def put(q, h, row, source):
        at = TILE + ((q % 2) * 2 + h) * half + row
        out[q // 2, pl.ds(pl.multiple_of(at, TILE), source.shape[0]), :] = source

    put(me, 0, 0, own[:half, :])
    put(me, 1, 0, own[half:, :])
    for h, parts in ((c, (mine_b, mine_a, mine_d0, mine_d1)), (1 - c, (other_b, other_a, other_d0, other_d1))):
        cut = parts[2].shape[0]
        put(me ^ 1, h, 0, parts[0][...])
        put(me ^ 2, h, 0, parts[1][...])
        put(me ^ 3, h, 0, parts[2][...])
        put(me ^ 3, h, cut, parts[3][:cut, :])
    a = me // 2
    out[1 - a, :TILE, :] = mine_d1[cut:, :]

    @pl.when(me % 2 == 0)
    def _():
        out[a, :TILE, :] = halo0[...]

    @pl.when(me % 2 == 1)
    def _():
        out[a, :TILE, :] = halo1[...]


def place_parts(weights, marks, rows, parts, info, layout):
    width = parts[0].shape[1]
    lane = lax.broadcasted_iota(jnp.int32, (TILE, LANES), 1) // TILE
    for (s, dy, first), part in zip(marks, parts):
        count = part.shape[0] // rows
        for k in range(count):
            block = layout[stored_block(s, dy, first + k, info)]
            at = pl.multiple_of(block * rows, TILE)
            weights[pl.ds(at, rows), :width] = part[k * rows : (k + 1) * rows, :]
        base = count * rows
        if part.shape[0] == base:
            continue
        for place in range(8):
            block = layout[stored_block(s, dy, place, info)]
            for piece in range(rows // TILE):
                packed = part[base : base + TILE, piece * LANES : (piece + 1) * LANES]
                kept = jnp.where(lane == place, packed, jnp.zeros_like(packed))
                at = pl.multiple_of(block * rows + piece * TILE, TILE)
                weights[pl.ds(at, TILE), width:] = kept


def weights_kernel(sizes, marks, rows, *refs):
    info, layout = views(refs[0], sizes)[:2]
    place_parts(refs[1 + len(marks)], marks, rows, refs[1 : 1 + len(marks)], info, layout)


def inner_kernel(hidden, weights, raw_ref, shared_ref, step_ref):
    bc = raw_ref.shape[2]
    for run in range(2):
        result = dot(hidden[run], weights[:, bc:])
        shared_ref[run] = result[:, :LANES].astype(BF16)
        step = result[:, LANES:]
        for shift in (64, 32, 16):
            step = step + pltpu.roll(step, shift, 1)
        step_ref[run] = step
        raw_ref[run] = dot(hidden[run], weights[:, :bc]).astype(BF16)


def gate_kernel(hidden, weights, gate_ref):
    for run in range(2):
        gate_ref[run] = jax.nn.silu(dot(hidden[run], weights[...])).astype(BF16)


def starts_of(lengths):
    starts, total = [], jnp.int32(0)
    for k in range(lengths.size):
        starts.append(total)
        total = total + lengths[k]
    return starts


def head_lanes(row, heads, info):
    return pltpu.roll(row, lax.rem(LANES - info[0] * heads, LANES), 1)


def chunk_start(i, info, tokens):
    t, y = info[3], info[4]
    per = tokens // PAGE
    q = i // per
    seq = ((t * 2 + q // 2) * 2 + y) * 2 + q % 2
    return seq * tokens + (i % per) * PAGE


def last_start(position, starts):
    best = jnp.int32(0)
    for k in range(len(starts)):
        best = jnp.maximum(best, jnp.where(starts[k] <= position, starts[k], 0))
    return best


def first_positions(first, starts, dims):
    position = first + lax.broadcasted_iota(jnp.int32, dims, 0)
    best = jnp.zeros(dims, jnp.int32)
    for k in range(len(starts)):
        best = jnp.maximum(best, jnp.where(starts[k] <= position, starts[k], 0))
    return best


def conv_silu(window, taps, bias, offset):
    total = bias + taps[0:1, :] * window[TILE : TILE + PAGE]
    for lag in range(1, CONV):
        within = (offset >= lag).astype(F32)
        total = total + taps[lag : lag + 1, :] * window[TILE - lag : TILE - lag + PAGE] * within
    return total / (1.0 + jnp.exp(-total))


def pair_columns(values, pair):
    lane = lax.broadcasted_iota(jnp.int32, (PAGE, LANES), 1)
    left = values[:, 2 * pair : 2 * pair + 1]
    right = values[:, 2 * pair + 1 : 2 * pair + 2]
    return jnp.where(lane < 64, left, right)


def state_kernel(heads, tokens, sizes, ints, raw, own, other, step, params, init, x_ref, b_ref, c_ref,
                 cum_ref, dt_ref, end_ref, factor_ref, summary_ref):
    info, _, lengths, groups = views(ints, sizes)[:4]
    starts = starts_of(lengths)
    width = heads * 64
    here = pl.ds(pl.multiple_of(info[0] * width, LANES), width)
    taps, bias = params[0:4, here], params[4:5, here]
    taps2, bias2 = params[8:12, : 2 * N], params[12:13, : 2 * N]
    per_head = head_lanes(params[8:16, 2 * N : 2 * N + LANES], heads, info)
    dt_bias, rate = per_head[0:1], -jnp.exp(per_head[1:2])
    chunks = x_ref.shape[0]
    per_run = chunks // 2
    pairs = heads // 2
    row = lax.broadcasted_iota(jnp.int32, (PAGE, PAGE), 0)
    col = lax.broadcasted_iota(jnp.int32, (PAGE, PAGE), 1)
    below = (row >= col).astype(F32)

    def one(i, carry):
        first = chunk_start(i, info, tokens)
        opened = last_start(first + PAGE - 1, starts)
        alive = (opened < first).astype(F32)
        start_of = first_positions(first, starts, (PAGE, 1))
        offset = first + lax.broadcasted_iota(jnp.int32, (PAGE, 1), 0) - start_of
        q = i // per_run
        at = pl.multiple_of((i % per_run) * PAGE, TILE)
        window = pl.ds(at, PAGE + TILE)
        x = conv_silu(raw[q, window, :].astype(F32), taps, bias, offset)
        is_first = info[1] == 0
        mine, theirs = own[q, window, :].astype(F32), other[q, window, :].astype(F32)
        b_raw = jnp.where(is_first, mine, theirs)
        c_raw = jnp.where(is_first, theirs, mine)
        b = conv_silu(b_raw, taps2[:, :LANES], bias2[:, :LANES], offset).astype(BF16)
        c = conv_silu(c_raw, taps2[:, LANES:], bias2[:, LANES:], offset).astype(BF16)
        raw_step = step[q, pl.ds(pl.multiple_of(at + TILE, TILE), PAGE), :]
        v = raw_step + dt_bias
        dt = jnp.maximum(v, 0.0) + jnp.log1p(jnp.exp(-jnp.abs(v)))
        log_rate = rate * dt
        cum = dot(below, log_rate, precision=HIGHEST)
        last = cum[PAGE - 1 : PAGE, :]
        kept = (row >= opened - first).astype(F32)
        weight = jnp.exp(last - cum) * dt * kept
        cum_t = cum.T
        x_ref[i] = x.astype(BF16)
        b_ref[i] = b
        c_ref[i] = c
        cum_ref[i] = cum
        dt_ref[i] = dt
        last_t = cum_t[0:8, PAGE - 1 : PAGE]
        factor_ref[i] = jnp.broadcast_to(jnp.exp(last_t), (8, LANES)) * alive
        for pair in range(pairs):
            here = slice(pair * LANES, (pair + 1) * LANES)
            scaled = (x[:, here] * pair_columns(weight, pair)).astype(BF16)
            end_ref[i, here, :] = dot(scaled, b, TN)

        @pl.when(opened >= first)
        def _():
            for k in range(len(starts)):

                @pl.when(starts[k] == opened)
                def _():
                    at_start = col == opened - first - 1
                    before = jnp.sum(jnp.where(at_start, cum_t, 0.0), axis=1, keepdims=True)
                    opening = jnp.broadcast_to(jnp.exp(last_t - before[0:8]), (8, LANES))
                    for h in range(heads):
                        here = slice(h * 64, (h + 1) * 64)
                        entered = opening[h : h + 1, :] * init[groups[k], here, :]
                        end_ref[i, here, :] = end_ref[i, here, :] + entered

        return carry

    lax.fori_loop(0, chunks, one, 0, unroll=4)
    for run in range(2):
        factor = factor_ref[run * per_run]
        for i in range(run * per_run + 1, (run + 1) * per_run):
            for h in range(heads):
                here = slice(h * 64, (h + 1) * 64)
                end_ref[i, here, :] = end_ref[i, here, :] + factor_ref[i, h : h + 1, :] * end_ref[i - 1, here, :]
            factor = factor * factor_ref[i]
            factor_ref[i] = factor
        summary_ref[run, : heads * 64, :] = end_ref[(run + 1) * per_run - 1].astype(BF16)
        tail = jnp.concatenate([factor, jnp.zeros_like(factor)], axis=0)
        summary_ref[run, heads * 64 :, :] = tail.astype(BF16)


def within_kernel(heads, tokens, sizes, ints, x_ref, b_ref, c_ref, cum_ref, dt_ref, params, init, y_ref):
    info, _, lengths, groups = views(ints, sizes)[:4]
    starts = starts_of(lengths)
    skip = head_lanes(params[8:16, 2 * N : 2 * N + LANES], heads, info)[2:3]
    skip = jnp.broadcast_to(skip, (PAGE, LANES))
    chunks = x_ref.shape[0]
    pairs = heads // 2
    row = lax.broadcasted_iota(jnp.int32, (PAGE, PAGE), 0)
    col = lax.broadcasted_iota(jnp.int32, (PAGE, PAGE), 1)
    lane = lax.broadcasted_iota(jnp.int32, (PAGE, LANES), 1)

    def one(i, carry):
        first = chunk_start(i, info, tokens)
        start_of = first_positions(first, starts, (PAGE, PAGE))
        bias = jnp.where((row >= col) & (col >= start_of - first), 0.0, -1e30)
        b, c = b_ref[i], c_ref[i]
        cum, dt = cum_ref[i], dt_ref[i]
        cum_t = cum.T
        scores = dot(c, b, NT)
        for pair in range(pairs):
            here = slice(pair * LANES, (pair + 1) * LANES)
            x = x_ref[i, :, here].astype(F32)
            scaled = x * pair_columns(dt, pair)
            mixing = []
            for h in (2 * pair, 2 * pair + 1):
                gap = cum[:, h : h + 1] + bias - cum_t[h : h + 1, :]
                mixing.append((scores * jnp.exp(gap)).astype(BF16))
            both = jnp.concatenate(
                [jnp.where(lane < 64, scaled, 0.0), jnp.where(lane < 64, 0.0, scaled)], axis=0
            ).astype(BF16)
            y = dot(jnp.concatenate(mixing, axis=1), both)
            y_ref[i, :, here] = y + pair_columns(skip, pair) * x
        @pl.when(last_start(first + PAGE - 1, starts) >= first)
        def _():
            for k in range(len(starts)):
                start = starts[k]

                @pl.when((start >= first) & (start < first + PAGE))
                def _():
                    at_start = row == start - first - 1
                    before = jnp.sum(jnp.where(at_start, cum, 0.0), axis=0, keepdims=True)
                    opening = jnp.exp(jnp.minimum(cum - before, 0.0))
                    opening = jnp.where(start_of == start, opening, 0.0)
                    for pair in range(pairs):
                        here = slice(pair * LANES, (pair + 1) * LANES)
                        read = dot(c, init[groups[k], here, :].astype(BF16), NT)
                        y_ref[i, :, here] = y_ref[i, :, here] + pair_columns(opening, pair) * read

        return carry

    lax.fori_loop(0, chunks, one, 0, unroll=4)


def onto(run, h, before):
    here = slice(h * 64, (h + 1) * 64)
    decay = run[run.shape[0] - 16 + h : run.shape[0] - 16 + h + 1, :].astype(F32)
    return decay * before + run[here, :].astype(F32)


def compose_kernel(heads, sizes, ints, mine, theirs, block_ref):
    info = views(ints, sizes)[0]
    low = info[4] == 0
    runs = []
    for a in range(2):
        m, q = mine[a].astype(F32), theirs[a].astype(F32)
        runs += [jnp.where(low, m, q), jnp.where(low, q, m)]
    total = runs[0]
    for run in runs[1:]:
        parts = []
        for h in range(heads):
            parts.append(onto(run, h, total[h * 64 : (h + 1) * 64, :]))
        tail = total[heads * 64 :, :] * run[heads * 64 :, :]
        total = jnp.concatenate(parts + [tail], axis=0)
    block_ref[...] = total.astype(BF16)


def enter_kernel(heads, tokens, sizes, ints, mine, theirs, entering, end_ref, factor_ref, states,
                 page0, page1, page2, page3, starting):
    info = views(ints, sizes)[0]
    me, y = info[0], info[4]
    per = tokens // PAGE
    per_run = states.shape[0] // 2
    for h in range(heads):
        here = slice(h * 64, (h + 1) * 64)
        outside = entering[here, :].astype(F32)
        first = jnp.where(y == 0, outside, onto(theirs[0], h, outside))
        starting[0, here, :] = first
        second = onto(mine[0], h, first)
        third = jnp.where(y == 0, onto(theirs[0], h, second), onto(theirs[1], h, second))
        starting[1, here, :] = third
    states[0] = starting[0].astype(BF16)
    states[per_run] = starting[1].astype(BF16)
    for rel, page in enumerate((page0, page1, page2, page3)):
        for k in range(per):
            i = (me ^ rel) * per + k
            run = i // per_run
            for h in range(heads):
                here = slice(h * 64, (h + 1) * 64)
                after = end_ref[i, here, :] + factor_ref[i, h : h + 1, :] * starting[run, here, :]
                page[k, here, :] = after.astype(BF16)

            @pl.when(i % per_run < per_run - 1)
            def _():
                states[i + 1] = page[k]


def finish_kernel(heads, tokens, sizes, ints, states, c_ref, cum_ref, y_ref, gate, params, mixed_ref,
                  square_ref):
    info, _, lengths = views(ints, sizes)[:3]
    starts = starts_of(lengths)
    width = heads * 64
    gain = params[5:6, pl.ds(pl.multiple_of(info[0] * width, LANES), width)]
    chunks = c_ref.shape[0]
    per_run = chunks // 2
    pairs = heads // 2
    ones = jnp.ones((8, LANES), F32)

    def one(i, carry):
        run = i // per_run
        first = chunk_start(i, info, tokens)
        alive = (first_positions(first, starts, (PAGE, LANES)) < first).astype(F32)
        decay = jnp.exp(cum_ref[i]) * alive
        read = dot(c_ref[i], states[i], NT)
        rows = pl.ds(pl.multiple_of(TILE + (i % per_run) * PAGE, TILE), PAGE)
        squares = jnp.zeros((PAGE, LANES), F32)
        for pair in range(pairs):
            here = slice(pair * LANES, (pair + 1) * LANES)
            value = y_ref[i, :, here] + pair_columns(decay, pair) * read[:, here]
            value = value * gate[run, rows, here].astype(F32)
            mixed_ref[i, :, here] = (value * gain[:, here]).astype(BF16)
            squares = squares + value * value
        square_ref[i] = dot(ones, squares, NT, HIGHEST)
        return carry

    lax.fori_loop(0, chunks, one, 0, unroll=4)


def columns_kernel(sizes, count, rows, ints, *refs):
    info = views(ints, sizes)[0]
    parts, out = refs[:count], refs[count]
    for index, part in enumerate(parts):
        for rel in range(4):
            seq = stored_block(index // 2, index % 2, 2 * (info[0] ^ rel), info) // 2
            at = pl.multiple_of(seq * rows, TILE)
            out[pl.ds(at, rows), :] = part[rel * rows : (rel + 1) * rows, :]


def mix_kernel(sizes, keep, ints, mixed, squares, columns, out):
    info = views(ints, sizes)[0]
    me, c = info[0], info[1]
    half = c if keep else 1 - c
    for rel in range(4):
        i = (me ^ rel) * 2 + half
        out[rel, :PAGE, :] = dot(mixed[i], columns[...], NT).astype(BF16)
        both = jnp.concatenate([squares[i], squares[i]], axis=0)
        out[rel, PAGE:, :LANES] = both.astype(BF16)
        out[rel, PAGE:, LANES:] = jnp.zeros((TILE, out.shape[2] - LANES), BF16)


def add_cores_kernel(kept, got, send_b, send_a, keep_b, keep_a):
    mid = send_b.shape[2]
    for k in (0, 1):
        total = kept[2 * k + 1, :, :mid].astype(F32) + got[2 * k + 1, :, :mid].astype(F32)
        send_b[k] = total.astype(BF16)
        keep_b[k] = kept[2 * k, :, :mid].astype(F32) + got[2 * k, :, :mid].astype(F32)
        total = kept[k + 2, :PAGE, mid:].astype(F32) + got[k + 2, :PAGE, mid:].astype(F32)
        send_a[k] = total.astype(BF16)
        keep_a[k] = kept[k, :PAGE, mid:].astype(F32) + got[k, :PAGE, mid:].astype(F32)


def add_second_kernel(keep_b, got_b, keep_a, got_a, send_a, send_b, left, right):
    send_a[...] = (keep_b[1] + got_b[1].astype(F32)).astype(BF16)
    left[...] = keep_b[0] + got_b[0].astype(F32)
    send_b[...] = (keep_a[1] + got_a[1].astype(F32)).astype(BF16)
    right[...] = keep_a[0] + got_a[0].astype(F32)


def add_last_kernel(channels, left, got_left, right, got_right, out):
    mid = left.shape[1]
    squares = left[PAGE : PAGE + 1, :LANES] + got_left[PAGE:, :LANES].astype(F32)[0:1]
    row = lax.broadcasted_iota(jnp.int32, (PAGE, PAGE), 0)
    col = lax.broadcasted_iota(jnp.int32, (PAGE, PAGE), 1)
    squares = jnp.sum(jnp.where(row == col, squares, 0.0), axis=1, keepdims=True)
    scale = lax.rsqrt(squares / channels + EPSILON)
    out[:, :mid] = ((left[:PAGE] + got_left[:PAGE, :].astype(F32)) * scale).astype(BF16)
    out[:, mid:] = ((right[...] + got_right[...].astype(F32)) * scale).astype(BF16)


def page_kernel(sizes, ints, own, from_b, from_a, from_d, out):
    info, _, _, _, table = views(ints, sizes)
    me, seq, per = info[0], info[6], own.shape[0]
    for k in range(per):
        slot = table[k] - seq * per
        for rel, source in enumerate((own, from_b, from_a, from_d)):
            out[slot, me ^ rel] = source[k].astype(F32)


def round_t(x, count):
    return lax.ppermute(x, "t", [(i, (i + 1) % count) for i in range(count)])


def weight_parts(part, count):
    parts = []
    for s in range(count):
        part = round_t(part, count) if s > 0 else part
        parts += [part, swap(part, "y")]
    return parts


def in_order(parts, index):
    stacked = jnp.stack(parts)
    blocks = stacked.reshape((-1, stacked.shape[1] * len(parts) // index.shape[0], stacked.shape[2]))
    return jnp.zeros_like(blocks).at[index].set(blocks).reshape(-1, stacked.shape[2])


def on_device(
    hidden_in,
    gate_proj,
    inner_proj,
    small_proj,
    row_layout,
    conv_inner,
    conv_shared,
    bias_inner,
    bias_shared,
    dt_bias,
    decay_log,
    skip_gain,
    norm_gain,
    out_proj,
    prompt_lengths,
    group_map,
    init_states,
    page_table,
):
    tokens, model = hidden_in.shape
    rows = gate_proj.shape[0]
    half_heads = dt_bias.shape[0]
    heads = half_heads // 4
    inner = conv_inner.shape[1]
    head_dim = inner // half_heads
    width = heads * head_dim
    t_count = lax.axis_size("t")
    t, a, y, b, c = (lax.axis_index(name) for name in ("t", "a", "y", "b", "tp"))
    me = a * 2 + b
    seq = ((t * 2 + a) * 2 + y) * 2 + b
    info = jnp.stack([me, c, 0 * c, t, y, 0 * c + t_count, seq, 0 * c]).astype(jnp.int32)
    pieces = [info, row_layout, prompt_lengths, group_map, page_table]
    sizes = tuple(piece.shape[0] for piece in pieces)
    ints = jnp.concatenate(pieces)
    per_head = jnp.pad(jnp.stack([dt_bias, decay_log, skip_gain]), ((0, 5), (0, LANES - half_heads)))
    top = jnp.concatenate([conv_inner, bias_inner[None], norm_gain[None]])
    low = jnp.concatenate([conv_shared, bias_shared[None]])
    low = jnp.concatenate([jnp.pad(low, ((0, 3), (0, 0))), per_head], axis=1)
    params = jnp.concatenate(
        [jnp.pad(top, ((0, 2), (0, 0))), jnp.pad(low, ((0, 0), (0, inner - low.shape[1])))]
    )
    count = 2 * t_count

    wide = width + N + LANES
    aligned = rows % TILE == 0
    size = lax.axis_size(SEQ)
    half = tokens // 2
    inner_send = call(
        functools.partial(pack_kernel, heads),
        "pack_rows",
        shape((8, rows, wide + width), BF16),
        [inner_proj, small_proj, gate_proj],
        [
            *[pltpu.VMEM(x.shape, F32) for x in (inner_proj, small_proj, gate_proj)],
            pltpu.SemaphoreType.DMA((3,)),
        ],
        us=2,
        limit=56,
        fetch=True,
    )
    inner_got = lax.all_to_all(inner_send, GROUP, 0, 0, tiled=True)
    mine, tail = call(
        functools.partial(rows_kernel, sizes),
        "own_rows",
        (shape((half, model), BF16), shape((TILE, model), BF16)),
        [ints, hidden_in],
        [pltpu.SemaphoreType.DMA((2,))],
        after=[inner_send],
        limit=56,
        fetch=True,
    )
    mine_b, mine_a = swap(mine, "b"), swap(mine, "a")

    if aligned:
        part, low, high, gate_part = call(
            repack_kernel,
            "repack_inner",
            (
                shape((8 * rows + TILE, width + N), BF16),
                shape((5 * rows, width + N), BF16),
                shape(((8 - 5) * rows + TILE, width + N), BF16),
                shape((8 * rows, width), BF16),
            ),
            [inner_got],
        )
        marks, inner_parts = [(0, 0, 0), (0, 1, 0)], [part, swap(part, "y")]
        for s in range(1, t_count):
            low, high = round_t(low, t_count), round_t(high, t_count)
            marks += [(s, 0, 0), (s, 0, 5), (s, 1, 0), (s, 1, 5)]
            inner_parts += [low, high, swap(low, "y"), swap(high, "y")]
        ready = [part]
    else:
        marks = None
        index = [stored_block(s, dy, p, info) for s in range(t_count) for dy in (0, 1) for p in range(8)]
        index = row_layout[jnp.stack(index)]
        inner_got = inner_got.reshape(8 * rows, wide + width)
        inner_weights = in_order(weight_parts(inner_got[:, :wide], t_count), index)
        gate_part = inner_got[:, wide:]
        ready = high = None

    halo0 = lax.ppermute(tail, SEQ, [(i, i + 1) for i in range(1, size - 1, 2)])
    halo1 = lax.ppermute(tail, SEQ, [(i, i + 2) for i in range(1, size - 2, 2)])

    over_b, over_a = call(
        functools.partial(forward_kernel, sizes),
        "forward_rows",
        (shape((half // 2, model), BF16), shape((half // 2 + TILE, model), BF16)),
        [ints, mine_b, mine_a, halo0, halo1],
        after=ready or [],
    )
    mine_d0, mine_d1 = swap(over_b, "b"), swap(over_a, "a")
    rows_in = [mine_b, mine_a, mine_d0, mine_d1]
    if aligned:
        gate_part = call(copy_kernel, "gate_part", shape(gate_part.shape, BF16), [gate_part], after=[high])
    gate_parts = weight_parts(gate_part, t_count)
    across = [(i, i ^ 3) for i in range(4)]
    out_rows = out_proj.shape[1]
    out_send = call(
        functools.partial(pack_out_kernel, sizes),
        "pack_out",
        [shape((out_rows, width), BF16)] * 4,
        [ints, out_proj.T],
        after=inner_parts[1:2] if aligned else [],
    )
    out_got = [
        out_send[0],
        swap(out_send[1], "b"),
        swap(out_send[2], "a"),
        lax.ppermute(out_send[3], ("a", "b"), across),
    ]
    out_part = call(join_kernel, "out_part", shape((4 * out_rows, width), BF16), out_got)
    out_parts = weight_parts(out_part, t_count)
    hidden = call(
        functools.partial(assemble_kernel, sizes),
        "assemble_rows",
        shape((2, TILE + 2 * tokens, model), BF16),
        [ints, hidden_in, *rows_in, *[swap(x, "tp") for x in rows_in], halo0, halo1],
        after=[],
        us=2,
    )
    if aligned:
        inner_weights = call(
            functools.partial(weights_kernel, sizes, marks, rows),
            "inner_weights",
            shape((model, wide), BF16),
            [ints, *inner_parts],
            us=15,
        )
    long = TILE + 2 * tokens
    raw, shared, step = call(
        inner_kernel,
        "inner_projection",
        (
            shape((2, long, width), BF16),
            shape((2, long, LANES), BF16),
            shape((2, long, LANES), F32),
        ),
        [hidden, inner_weights],
        us=3.5,
    )
    shared_other = swap(shared, "tp")
    init = lax.dynamic_slice_in_dim(init_states, me * heads, heads, 1)
    init = init.reshape(init.shape[0], width, N)
    chunks = 4 * tokens // PAGE
    x, b_in, c_in, cum, dt, ends, factors, summary = call(
        functools.partial(state_kernel, heads, tokens, sizes),
        "states",
        (
            shape((chunks, PAGE, width), BF16),
            shape((chunks, PAGE, N), BF16),
            shape((chunks, PAGE, N), BF16),
            shape((chunks, PAGE, LANES), F32),
            shape((chunks, PAGE, LANES), F32),
            shape((chunks, width, N), F32),
            shape((chunks, 8, N), F32),
            shape((2, width + 16, N), BF16),
        ),
        [ints, raw, shared, shared_other, step, params, init],
        after=gate_parts[2:3],
        us=7,
    )
    if aligned:
        gate_marks = [(s, dy, 0) for s in range(t_count) for dy in (0, 1)]
        gate_weights = call(
            functools.partial(weights_kernel, sizes, gate_marks, rows),
            "gate_weights",
            shape((model, width), BF16),
            [ints, *gate_parts],
            after=[summary],
            us=1,
        )
    else:
        gate_weights = in_order(gate_parts, index)
    if out_rows % TILE == 0:
        columns = call(
            functools.partial(columns_kernel, sizes, count, out_rows),
            "columns",
            shape((model, width), BF16),
            [ints, *out_parts],
            after=[summary],
            us=1,
        )
    else:
        index = [
            stored_block(s, dy, 2 * (me ^ rel), info) // 2
            for s in range(t_count)
            for dy in (0, 1)
            for rel in range(4)
        ]
        columns = in_order(out_parts, jnp.stack(index))
    theirs = swap(summary, "y")
    block = call(
        functools.partial(compose_kernel, heads, sizes),
        "compose",
        shape((width + 16, N), BF16),
        [ints, summary, theirs],
    )
    composed = block
    onward = [(i, i + 1) for i in range(t_count - 1)]
    block = lax.ppermute(block, "t", onward)
    entering = block
    if t_count > 2:
        total = block[:width].astype(F32).reshape(heads, head_dim, N)
        decay = block[width : width + heads, None, :].astype(F32)
        for _ in range(t_count - 2):
            block = lax.ppermute(block, "t", onward)
            total = total + decay * block[:width].astype(F32).reshape(heads, head_dim, N)
            decay = decay * block[width : width + heads, None, :].astype(F32)
        entering = total.reshape(width, N)
    y_within = call(
        functools.partial(within_kernel, heads, tokens, sizes),
        "within_chunks",
        shape((chunks, PAGE, width), F32),
        [ints, x, b_in, c_in, cum, dt, params, init],
        after=[composed, out_parts[2]],
        us=5,
    )
    states, *pages = call(
        functools.partial(enter_kernel, heads, tokens, sizes),
        "entering_states",
        (shape((chunks, width, N), BF16), *[shape((tokens // PAGE, width, N), BF16)] * 4),
        [ints, summary, theirs, entering, ends, factors],
        [pltpu.VMEM((2, width, N), F32)],
    )
    got_pages = [pages[0], swap(pages[1], "b"), swap(pages[2], "a"), lax.ppermute(pages[3], ("a", "b"), across)]
    gate = call(
        gate_kernel,
        "gate_projection",
        shape((2, long, width), BF16),
        [hidden, gate_weights],
        after=[states],
        us=2.5,
    )
    mixed, squares = call(
        functools.partial(finish_kernel, heads, tokens, sizes),
        "finish",
        (shape((chunks, PAGE, width), BF16), shape((chunks, 8, PAGE), F32)),
        [ints, states, c_in, cum, y_within, gate, params],
        after=got_pages[1:2],
        us=4,
    )

    dims = shape((4, PAGE + TILE, model), BF16)
    sent = call(functools.partial(mix_kernel, sizes, False), "mix_send", dims, [ints, mixed, squares, columns],
                after=got_pages[2:4], us=2.1)
    mix_sent = sent
    got = swap(sent, "tp")
    kept = call(functools.partial(mix_kernel, sizes, True), "mix_keep", dims, [ints, mixed, squares, columns],
                after=[mix_sent], us=2.1)
    mid = model // 2
    send_b, send_a, keep_b, keep_a = call(
        add_cores_kernel,
        "add_cores",
        (
            shape((2, PAGE + TILE, mid), BF16),
            shape((2, PAGE, mid), BF16),
            shape((2, PAGE + TILE, mid), F32),
            shape((2, PAGE, mid), F32),
        ),
        [kept, got],
    )
    per = tokens // PAGE
    state_pages = call(
        functools.partial(page_kernel, sizes), "pages", shape((per, 4, width, N), F32), [ints, *got_pages], after=[send_b], us=1.8
    )

    got_b, got_a = swap(send_b, "b"), swap(send_a, "a")
    send_a, send_b, left, right = call(
        add_second_kernel,
        "add_second",
        (
            shape((PAGE + TILE, mid), BF16),
            shape((PAGE, mid), BF16),
            shape((PAGE + TILE, mid), F32),
            shape((PAGE, mid), F32),
        ),
        [keep_b, got_b, keep_a, got_a],
    )
    got_left, got_right = swap(send_a, "a"), swap(send_b, "b")
    mixed_out = call(
        functools.partial(add_last_kernel, float(2 * inner)),
        "add_last",
        shape((PAGE, model), BF16),
        [left, got_left, right, got_right],
    )
    return (mixed_out, state_pages.reshape(per, half_heads, head_dim, N))


def solution(mesh):
    count = mesh.shape["seq"]
    fine = Mesh(mesh.devices.reshape(count // 8, 2, 2, 2, 2), SEQ + ("tp",))
    placed = (
        P(SEQ, None),
        P(SEQ + ("tp",), None),
        P(SEQ + ("tp",), None),
        P(SEQ + ("tp",), None),
        P(),
        P(None, "tp"),
        P(),
        P("tp"),
        P(),
        P("tp"),
        P("tp"),
        P("tp"),
        P("tp"),
        P("tp", SEQ),
        P(),
        P(),
        P(None, "tp", None, None),
        P(SEQ),
    )
    return jax.shard_map(
        on_device,
        mesh=fine,
        in_specs=placed,
        out_specs=(P(SEQ + ("tp",), None), P(SEQ, "tp", None, None)),
        check_vma=False,
    )
```
